128 devices in a mesh: lon: 32 (over y, z, x_lo), lat: 4 (over x_hi, core).
Axes of the slice: x: 4 (x_hi: 2, x_lo: 2; x = x_hi * 2 + x_lo), y: 4, z: 4, core: 2. Of those that a mesh axis runs over, the one named last changes fastest.
Arguments:
- adjoint_final: float32 [75, 32, 8192], P(None, 'lat', 'lon'), may hold values from -6 to 6
- vert_inverse: bfloat16 [75, 75, 32, 8192], P(None, None, 'lat', 'lon'), may hold values from -0.36 to 1
- speed_east: bfloat16 [75, 32, 8192], P(None, 'lat', 'lon'), may hold values from -0.3984375 to 0.3984375
- mixing_east: bfloat16 [75, 32, 8192], P(None, 'lat', 'lon'), may hold values from 0.019897461 to 0.119628906
- speed_north: bfloat16 [75, 32, 8192], P(None, 'lat', 'lon'), may hold values from -0.3984375 to 0.3984375
- mixing_north: bfloat16 [75, 32, 8192], P(None, 'lat', 'lon'), may hold values from 0.019897461 to 0.119628906
- depth_levels: int32 [32, 8192], P('lat', 'lon'), may hold values from 0 to 75
- fold_block: int32 [32], replicated, may hold values from 0 to 31, as said below
Outputs:
- adjoint_initial: float32 [75, 32, 8192], P(None, 'lat', 'lon')
The draws below stay inside these ranges and needn't reach their ends.
Inputs may be any that keep to these rules, and one draw needn't show every extreme that they name: fold_block pairs the longitude blocks: fold_block[fold_block[b]] = b and fold_block[b] != b.
All inputs are finite; a program needn't handle non-finite values.
Results may differ from the reference program's by a relative error of at most 0.0005.
Values may be sent and summed in bfloat16 or wider, within the bound.
No kernel may reach another device: no remote copies, remote signals or barrier semaphores. Data moves between devices by JAX's collectives and lax.ppermute only.
A program may use at most 128 MiB of HBM per device.

```python
import jax
import jax.numpy as jnp
from jax import lax

LEV = 75
CLON = 256
STEPS = 2
NLAT = 32
NLON = 8192
N_LON = 32


def draw_vert_inverse(key, part):
    key = jax.random.fold_in(key, 11)
    diag_low = 0.55
    reach_len = 6.0

    def one_level(level_row):
        level_key = jax.random.fold_in(key, level_row)
        off_noise = jax.random.uniform(level_key, (LEV, NLAT, NLON), jnp.float32, -1.0, 1.0)
        diag_noise = jax.random.uniform(jax.random.fold_in(level_key, 1), (LEV, NLAT, NLON), jnp.float32, diag_low, 1.0)
        distance = jnp.abs(jnp.arange(LEV, dtype=jnp.int32) - level_row).astype(jnp.float32)[:, None, None]
        coupling = 0.35 * off_noise * jnp.exp(-distance / reach_len)
        return jnp.where(distance == 0.0, diag_noise, coupling).astype(jnp.bfloat16)
    return lax.map(one_level, jnp.arange(LEV, dtype=jnp.int32))


def draw_fold_block(key, part):
    key = jax.random.fold_in(key, 7)
    half_loop = N_LON // 2
    start_block = jax.random.randint(jax.random.fold_in(key, 1), (), 0, half_loop).astype(jnp.int32)
    blocks = jnp.arange(N_LON, dtype=jnp.int32)
    excluded = (blocks == start_block) | (blocks == start_block + half_loop)
    ranks = jax.random.permutation(jax.random.fold_in(key, 2), N_LON).astype(jnp.int32)
    scores = jnp.where(excluded, ranks + N_LON, ranks)
    order = jnp.argsort(scores).astype(jnp.int32)
    evens = order[0::2]
    odds = order[1::2]
    paired = jnp.zeros((N_LON,), jnp.int32).at[evens].set(odds)
    return paired.at[odds].set(evens)


def set_ends(result, stream_key, low, top_value):
    longest = result.shape.index(max(result.shape))
    spots = []
    for shift in (0, 1):
        where = [jax.random.randint(jax.random.fold_in(stream_key, axis), (), 0, length) for axis, length in enumerate(result.shape)]
        where[longest] = (where[longest] + shift) % result.shape[longest]
        spots.append(tuple(where))
    return result.at[spots[0]].set(low).at[spots[1]].set(top_value)


def block_scale(rng, dims, cuts, smallest, largest):
    def one(axis_at, blocks):
        heights = jax.random.uniform(jax.random.fold_in(jax.random.fold_in(rng, 6), axis_at), (blocks,), jnp.float32, smallest / len(cuts), largest / len(cuts))
        return jnp.repeat(jnp.exp(heights), dims[axis_at] // blocks).reshape((-1,) + (1,) * (len(dims) - axis_at - 1))

    level = one(*cuts[0])
    for cut in cuts[1:]:
        level = level * one(*cut)
    return level


def gaussian(own_key, extent, scale, limit, split=(), kind=jnp.bfloat16):
    array = jax.random.normal(own_key, extent, jnp.float32) * scale
    if len(split) > 0:
        array = block_scale(own_key, extent, split, -0.22, 0.18) * array
    return jnp.clip(array, min=-limit, max=limit).astype(kind)


def setup_inputs(seed: int = 0) -> dict:
    key_of = jax.random.split(jax.random.key(seed), 9)
    adjoint_final = gaussian(key_of[0], (LEV, NLAT, NLON), 1.0, 6.0, ((1, 4), (2, 32)), jnp.float32)
    vert_inverse = draw_vert_inverse(jax.random.fold_in(key_of[8], 71), 0)
    speed_east = jnp.clip(jax.random.uniform(key_of[2], (LEV, NLAT, NLON), jnp.float32, -0.3984375, 0.3984375) * block_scale(key_of[2], (LEV, NLAT, NLON), ((1, 4), (2, 32)), -0.4, 0.0), -0.3984375, 0.3984375).astype(jnp.bfloat16)
    mixing_east = jnp.clip(0.019897461 + 0.099731445 * jax.random.uniform(key_of[3], (LEV, NLAT, NLON), jnp.float32) ** block_scale(key_of[3], (LEV, NLAT, NLON), ((1, 4), (2, 32)), -0.2, 0.2), 0.019897461, 0.119628906).astype(jnp.bfloat16)
    speed_north = jnp.clip(jax.random.uniform(key_of[4], (LEV, NLAT, NLON), jnp.float32, -0.3984375, 0.3984375) * block_scale(key_of[4], (LEV, NLAT, NLON), ((1, 4), (2, 32)), -0.4, 0.0), -0.3984375, 0.3984375).astype(jnp.bfloat16)
    mixing_north = jnp.clip(0.019897461 + 0.099731445 * jax.random.uniform(key_of[5], (LEV, NLAT, NLON), jnp.float32) ** block_scale(key_of[5], (LEV, NLAT, NLON), ((1, 4), (2, 32)), -0.2, 0.2), 0.019897461, 0.119628906).astype(jnp.bfloat16)
    depth_levels = set_ends(jax.random.randint(key_of[6], (NLAT, NLON), 0, LEV + 1), jax.random.fold_in(key_of[6], 1), 0, LEV).astype(jnp.int32)
    fold_block = draw_fold_block(jax.random.fold_in(key_of[8], 71), 0)
    return dict(adjoint_final=adjoint_final, vert_inverse=vert_inverse, speed_east=speed_east, mixing_east=mixing_east, speed_north=speed_north, mixing_north=mixing_north, depth_levels=depth_levels, fold_block=fold_block)


def partner_columns(fold_block):
    columns = jnp.arange(NLON, dtype=jnp.int32)
    return fold_block[columns // CLON] * CLON + (CLON - 1 - columns % CLON)

def extend(field_data, partner):
    south_rows = jnp.zeros((field_data.shape[0], 2, field_data.shape[2]), jnp.float32)
    first_ghost = jnp.take(field_data[:, NLAT - 2, :], partner, axis=1)
    second = jnp.take(field_data[:, NLAT - 3, :], partner, axis=1)
    with_rows = jnp.concatenate([south_rows, field_data, first_ghost[:, None, :], second[:, None, :]], axis=1)
    return jnp.concatenate([with_rows[:, :, -2:], with_rows, with_rows[:, :, :2]], axis=2)

def face_flux(strip_cells, speed_face, mixing, flux_axis):
    cell_count = strip_cells.shape[flux_axis]
    far_low = lax.slice_in_dim(strip_cells, 0, cell_count - 3, axis=flux_axis)
    near_low = lax.slice_in_dim(strip_cells, 1, cell_count - 2, axis=flux_axis)
    near_high = lax.slice_in_dim(strip_cells, 2, cell_count - 1, axis=flux_axis)
    far_high = lax.slice_in_dim(strip_cells, 3, cell_count, axis=flux_axis)
    return speed_face * (7.0 * (near_low + near_high) - far_low - far_high) / 12.0 - mixing * (near_high - near_low)

def horizontal(tracer, wet_mask, partner, speed_x, mixing_x, speed_y, mixing_y):
    extended = extend(wet_mask * tracer, partner)
    flux_x = face_flux(extended[:, 2:-2, :], speed_x, mixing_x, 2)
    flux_y = face_flux(extended[:, :, 2:-2], speed_y, mixing_y, 1)
    centre = extended[:, 2:-2, 2:-2]
    return wet_mask * (centre - (flux_x[:, :, 1:] - flux_x[:, :, :-1]) - (flux_y[:, 1:, :] - flux_y[:, :-1, :]))

def vertical_adjoint(vert_inverse, weighted):

    def one_row(lat_row):
        row_block = lax.dynamic_index_in_dim(vert_inverse, lat_row, 2, keepdims=False).astype(jnp.float32)
        row_vector = lax.dynamic_index_in_dim(weighted, lat_row, 1, keepdims=False)
        return jnp.einsum('kjx,kx->jx', row_block, row_vector, precision=lax.Precision.HIGHEST)
    stacked = lax.map(one_row, jnp.arange(NLAT, dtype=jnp.int32))
    return jnp.transpose(stacked, (1, 0, 2))

def reference(adjoint_final, vert_inverse, speed_east, mixing_east, speed_north, mixing_north, depth_levels, fold_block):
    wet_mask = (jnp.arange(LEV, dtype=jnp.int32)[:, None, None] < depth_levels[None]).astype(jnp.float32)
    partner = partner_columns(fold_block)
    speed_x = jnp.concatenate([speed_east[:, :, -1:], speed_east], axis=2).astype(jnp.float32)
    mixing_x = jnp.concatenate([mixing_east[:, :, -1:], mixing_east], axis=2).astype(jnp.float32)
    zero_row = jnp.zeros((LEV, 1, NLON), jnp.float32)
    speed_y = jnp.concatenate([zero_row, speed_north.astype(jnp.float32)], axis=1)
    mixing_y = jnp.concatenate([zero_row, mixing_north.astype(jnp.float32)], axis=1)

    def operator(tracer):
        return horizontal(tracer, wet_mask, partner, speed_x, mixing_x, speed_y, mixing_y)
    primal_out, pullback = jax.vjp(operator, jnp.zeros((LEV, NLAT, NLON), jnp.float32))
    adjoint = adjoint_final
    for turn_index in range(STEPS):
        projected = vertical_adjoint(vert_inverse, wet_mask * adjoint)
        adjoint = pullback(projected)[0]
    return adjoint
```

```python
import jax
import jax.numpy as jnp
from jax import lax
from jax.experimental import pallas as pl
from jax.experimental.pallas import tpu as pltpu
from jax.sharding import PartitionSpec as P

F32 = jnp.float32
BF16 = jnp.bfloat16
LEV = 75
ROWS = 8
COLS = 256
HALF = 128
JB = 5
QUADS = 19
FULL_QUADS = 18
TAIL = LEV - 4 * FULL_QUADS
MIX_LANE = 22


def lane_ids():
    return lax.broadcasted_iota(jnp.int32, (ROWS, HALF), 1)


def row_ids():
    return lax.broadcasted_iota(jnp.int32, (ROWS, HALF), 0)


def turn(tile, shift, axis):
    size = tile.shape[axis]
    if isinstance(shift, int):
        shift = shift % size
        if shift == 0:
            return tile
    return pltpu.roll(tile, shift, axis)


def halves(value):
    return [value[:, :HALF], value[:, HALF:]]


def for_quads(body):
    def step(quad, carry):
        body(quad, 4)
        return carry

    lax.fori_loop(0, FULL_QUADS, step, 0)
    body(FULL_QUADS, TAIL)


def vertical_block(inverse_ref, weighted_ref, depth, first_level, g_ref):
    group = 15

    def some_levels(step, sums):
        sums = list(sums)
        for offset in range(group):
            k = step * group + offset
            weight = weighted_ref[k]
            for jj in range(JB):
                sums[jj] = sums[jj] + inverse_ref[k, jj].astype(F32) * weight
        return tuple(sums)

    zero = jnp.zeros((ROWS, COLS), F32)
    sums = lax.fori_loop(0, LEV // group, some_levels, (zero,) * JB)
    for jj in range(JB):
        j = first_level + jj
        g_ref[j] = jnp.where(depth > j, sums[jj], 0.0)


def place_lanes(acc_ref, side, j, tile, from_lane):
    spot = lax.rem(j, 64)
    which = j // 64
    rolled = pltpu.roll(tile, lax.rem(2 * spot + (2 * HALF - from_lane), HALF), 1)
    keep = (lane_ids() // 2) == spot
    acc_ref[side, which] = jnp.where(keep, rolled, acc_ref[side, which])


def place_mix(acc_ref, side, j, tile):
    lane = MIX_LANE + j
    rolled = pltpu.roll(tile, lax.rem(lane + 1, HALF), 1)
    acc_ref[side, 1] = jnp.where(lane_ids() == lane, rolled, acc_ref[side, 1])


def pack_rims(g_ref, sn_ref, mn_ref, se_ref, me_ref, slots_ref, north_ref, south_ref, lonc_ref,
              fold_scr, lon_scr, lonc_scr, with_coefs):
    row = row_ids()
    lon_scr[...] = jnp.zeros_like(lon_scr)
    if with_coefs:
        lonc_scr[...] = jnp.zeros_like(lonc_scr)
    fold_scr[...] = jnp.zeros_like(fold_scr)

    def quad_body(quad, count):
        zero = jnp.zeros((ROWS, HALF), F32)
        north = [zero, zero]
        south = [zero, zero]
        fold = [zero, zero]
        s_north = [zero, zero]
        m_north = [zero, zero]
        s_south = [zero, zero]
        for l in range(count):
            j = quad * 4 + l
            mine = (row // 2) == l
            g = halves(g_ref[j])
            s = halves(sn_ref[j].astype(F32))
            m = halves(mn_ref[j].astype(F32))
            for c in range(2):
                north[c] = jnp.where(mine, turn(g[c], 2 * l - 6, 0), north[c])
                south[c] = jnp.where(mine, turn(g[c], 2 * l, 0), south[c])
                slope = s[c] * (1.0 / 12.0)
                direct = g[c] * (m[c] - 7.0 * slope)
                inner = (g[c] - turn(g[c], -1, 0)) * slope
                both = jnp.where(row == 7, direct + turn(inner, 1, 0), turn(slope * g[c], -1, 0))
                fold[c] = jnp.where(mine, turn(both, 2 * l - 6, 0), fold[c])
                if with_coefs:
                    s_north[c] = jnp.where(mine, turn(s[c], 2 * l - 6, 0), s_north[c])
                    m_north[c] = jnp.where(mine, turn(m[c], 2 * l - 6, 0), m_north[c])
                    s_south[c] = jnp.where(mine, turn(s[c], 2 * l, 0), s_south[c])
            place_lanes(lon_scr, 0, j, g[1], 126)
            place_lanes(lon_scr, 1, j, g[0], 0)
            if with_coefs:
                se = halves(se_ref[j].astype(F32))
                me = halves(me_ref[j].astype(F32))
                place_lanes(lonc_scr, 0, j, se[1], 126)
                place_lanes(lonc_scr, 1, j, se[0], 0)
                place_mix(lonc_scr, 0, j, me[1])
        for c in range(2):
            cols = slice(c * HALF, (c + 1) * HALF)
            north_ref[0, quad, :, cols] = north[c].astype(BF16)
            south_ref[0, quad, :, cols] = south[c].astype(BF16)
            fold_scr[quad, :, cols] = fold[c]
            if with_coefs:
                north_ref[1, quad, :, cols] = s_north[c].astype(BF16)
                north_ref[2, quad, :, cols] = m_north[c].astype(BF16)
                south_ref[1, quad, :, cols] = s_south[c].astype(BF16)

    for_quads(quad_body)
    r = lax.broadcasted_iota(jnp.int32, (COLS, COLS), 0)
    q = lax.broadcasted_iota(jnp.int32, (COLS, COLS), 1)
    mirror = (r + q == COLS - 1).astype(F32).astype(BF16)
    flat = fold_scr[...].reshape(20 * ROWS, COLS).astype(BF16)
    flipped = jnp.dot(flat, mirror, preferred_element_type=F32).reshape(20, ROWS, COLS)
    count = lax.axis_size("lon")
    me_lon = lax.axis_index("lon")
    east = lax.rem(me_lon + 1, count)
    west = lax.rem(me_lon + count - 1, count)
    to_east = jnp.concatenate([lon_scr[0, 0], lon_scr[0, 1]], axis=1)
    to_west = jnp.concatenate([lon_scr[1, 0], lon_scr[1, 1]], axis=1)
    zero = jnp.zeros((ROWS, COLS), F32)
    for i in range(slots_ref.shape[0]):
        piece = flipped[i] if i < QUADS else zero
        rim = jnp.where(i == east, to_east, jnp.where(i == west, to_west, zero))
        slots_ref[i] = jnp.concatenate([piece, rim], axis=0).astype(BF16)
    if with_coefs:
        for side in range(2):
            lonc_ref[side] = jnp.concatenate([lonc_scr[side, 0], lonc_scr[side, 1]], axis=1).astype(BF16)


def transposed_h(g_ref, se_ref, me_ref, sn_ref, mn_ref, depth_ref, slots_ref, coef_slots_ref,
                 fold_slots_ref, north_ref, south_ref, north_c_ref, south_c_ref, out_ref):
    row = row_ids()
    lane = lane_ids()
    count = lax.axis_size("lon")
    me_lon = lax.axis_index("lon")
    east = lax.rem(me_lon + 1, count)
    west = lax.rem(me_lon + count - 1, count)
    lat = lax.axis_index("lat")
    has_south = (lat > 0).astype(F32)
    has_north = (lat < lax.axis_size("lat") - 1).astype(F32)
    is_top = 1.0 - has_north
    lon_w = slots_ref.at[west]
    lon_e = slots_ref.at[east]
    lonc_w = coef_slots_ref.at[west]
    lonc_e = coef_slots_ref.at[east]

    def pick(ref):
        value = ref[...].astype(F32)[ROWS:]
        return halves(value)

    gw, ge, cw, ce = pick(lon_w), pick(lon_e), pick(lonc_w), pick(lonc_e)

    def quad_body(quad, levels):
        g_n = halves(north_ref[0, quad].astype(F32) * has_south)
        s_n = halves(north_c_ref[1, quad].astype(F32) * has_south)
        m_n = halves(north_c_ref[2, quad].astype(F32) * has_south)
        g_s = halves(south_ref[0, quad].astype(F32) * has_north)
        s_s = halves(south_c_ref[1, quad].astype(F32) * has_north)
        fold = halves(fold_slots_ref[quad].astype(F32)[:ROWS] * is_top)
        for l in range(levels):
            j = quad * 4 + l
            depth = halves(depth_ref[...])
            g = halves(g_ref[j])
            se = halves(se_ref[j].astype(F32))
            me = halves(me_ref[j].astype(F32))
            sn = halves(sn_ref[j].astype(F32))
            mn = halves(mn_ref[j].astype(F32))
            first = j < 64
            at = 2 * lax.rem(j, 64)
            back = lax.rem(HALF - at, HALF)
            fore = lax.rem(2 * HALF - 2 - at, HALF)
            g_rim = jnp.where(
                lane < 64,
                pltpu.roll(jnp.where(first, ge[0], ge[1]), back, 1),
                pltpu.roll(jnp.where(first, gw[0], gw[1]), fore, 1),
            )
            s_rim = jnp.where(
                lane < 64,
                pltpu.roll(jnp.where(first, ce[0], ce[1]), back, 1),
                pltpu.roll(jnp.where(first, cw[0], cw[1]), fore, 1),
            )
            m_rim = pltpu.roll(cw[1], lax.rem(2 * HALF - 1 - MIX_LANE - j, HALF), 1)
            tiles = [g[0], g[1], g_rim]
            ahead = [turn(jnp.where(lane == 0, tiles[(c + 1) % 3], tiles[c]), -1, 1) for c in range(3)]
            jump = [ahead[c] - tiles[c] for c in range(3)]
            slope = [x * (1.0 / 12.0) for x in (se[0], se[1], s_rim)]
            mixes = [me[0], me[1], m_rim]
            far = [-slope[c] * jump[c] for c in range(3)]
            high = [(7.0 * slope[c] - mixes[c]) * jump[c] for c in range(3)]
            total = []
            for c in range(2):
                before = (c + 2) % 3
                after = c + 1
                value = g[c] + (7.0 * slope[c] + mixes[c]) * jump[c]
                value = value + turn(jnp.where(lane == 127, high[before], high[c]), 1, 1)
                value = value + turn(jnp.where(lane == 0, far[after], far[c]), -1, 1)
                value = value + turn(jnp.where(lane >= 126, far[before], far[c]), 2, 1)
                total.append(value)
            for c in range(2):
                rim = jnp.where(row < 4, turn(g_s[c], -2 * l, 0), turn(g_n[c], 6 - 2 * l, 0))
                s_r = jnp.where(row < 4, turn(s_s[c], -2 * l, 0), turn(s_n[c], 6 - 2 * l, 0)) * (1.0 / 12.0)
                m_r = turn(m_n[c], 6 - 2 * l, 0)
                d = turn(jnp.where(row == 0, rim, g[c]), -1, 0) - g[c]
                d_r = turn(jnp.where(row == 0, g[c], rim), -1, 0) - rim
                sl = sn[c] * (1.0 / 12.0)
                hi = (7.0 * sl - mn[c]) * d
                hi_r = (7.0 * s_r - m_r) * d_r
                fa = -sl * d
                fa_r = -s_r * d_r
                value = total[c] + (7.0 * sl + mn[c]) * d
                value = value + turn(jnp.where(row == 7, hi_r, hi), 1, 0)
                value = value + turn(jnp.where(row == 0, fa_r, fa), -1, 0)
                value = value + turn(jnp.where(row >= 6, fa_r, fa), 2, 0)
                over = turn(fold[c], 5 - 2 * l, 0)
                value = value + jnp.where((row == 5) | (row == 6), over, 0.0)
                out_ref[j, :, c * HALF:(c + 1) * HALF] = jnp.where(depth[c] > j, value, 0.0)

    for_quads(quad_body)


def first_kernel(lam_ref, inv_ref, se_ref, me_ref, sn_ref, mn_ref, depth_ref,
                 g_ref, slots_ref, north_ref, south_ref, lonc_ref,
                 weighted, fold_scr, lon_scr, lonc_scr):
    step = pl.program_id(0)
    depth = depth_ref[...]

    @pl.when(step == 0)
    def _():
        def mask(k, carry):
            weighted[k] = jnp.where(depth > k, lam_ref[k], 0.0)
            return carry

        lax.fori_loop(0, LEV, mask, 0, unroll=5)

    vertical_block(inv_ref, weighted, depth, step * JB, g_ref)

    @pl.when(step == pl.num_programs(0) - 1)
    def _():
        pack_rims(g_ref, sn_ref, mn_ref, se_ref, me_ref, slots_ref, north_ref, south_ref, lonc_ref,
                  fold_scr, lon_scr, lonc_scr, True)


def second_kernel(g1_ref, inv_ref, se_ref, me_ref, sn_ref, mn_ref, depth_ref,
                  in_slots_ref, coef_slots_ref, in_north_ref, in_south_ref,
                  g_ref, slots_ref, north_ref, south_ref, weighted, fold_scr, lon_scr):
    step = pl.program_id(0)

    @pl.when(step == 0)
    def _():
        transposed_h(g1_ref, se_ref, me_ref, sn_ref, mn_ref, depth_ref, in_slots_ref, coef_slots_ref,
                     coef_slots_ref, in_north_ref, in_south_ref, in_north_ref, in_south_ref, weighted)

    vertical_block(inv_ref, weighted, depth_ref[...], step * JB, g_ref)

    @pl.when(step == pl.num_programs(0) - 1)
    def _():
        pack_rims(g_ref, sn_ref, mn_ref, se_ref, me_ref, slots_ref, north_ref, south_ref, None,
                  fold_scr, lon_scr, None, False)


def relay_kernel(fold_ref, in_ref, lonc_ref, out_ref):
    count = out_ref.shape[0]
    me_lon = lax.axis_index("lon")
    east = lax.rem(me_lon + 1, count)
    west = lax.rem(me_lon + count - 1, count)
    for d in range(count):
        piece = in_ref[fold_ref[d]]
        if lonc_ref is None:
            out_ref[d] = piece
        else:
            rim = jnp.where(d == east, lonc_ref[0].astype(F32), lonc_ref[1].astype(F32))
            out_ref[d] = jnp.concatenate([piece.astype(F32)[:ROWS], rim], axis=0).astype(BF16)


def plain_relay(fold_ref, in_ref, out_ref):
    relay_kernel(fold_ref, in_ref, None, out_ref)


def third_kernel(g_ref, se_ref, me_ref, sn_ref, mn_ref, depth_ref, slots_ref, coef_slots_ref,
                 fold_slots_ref, north_ref, south_ref, north_c_ref, south_c_ref, out_ref):
    transposed_h(g_ref, se_ref, me_ref, sn_ref, mn_ref, depth_ref, slots_ref, coef_slots_ref,
                 fold_slots_ref, north_ref, south_ref, north_c_ref, south_c_ref, out_ref)


def whole(shape):
    zeros = (0,) * len(shape)
    return pl.BlockSpec(shape, lambda *_: zeros)


def shaped(shape, dtype):
    return jax.ShapeDtypeStruct(shape, dtype)


def per_device(lam, inverse, se, me, sn, mn, depth, fold_block):
    field = (LEV, ROWS, COLS)
    count = lax.axis_size("lon")
    lats = lax.axis_size("lat")
    slot_shape = (count, 2 * ROWS, COLS)
    params = pltpu.CompilerParams(vmem_limit_bytes=40 * 1024 * 1024)
    vspec = pl.BlockSpec((LEV, JB, ROWS, COLS), lambda b: (0, b, 0, 0))
    grid = (LEV // JB,)
    coefs = [se, me, sn, mn]
    cost = pl.CostEstimate(flops=2 * LEV * LEV * ROWS * COLS, bytes_accessed=LEV * LEV * ROWS * COLS * 2,
                           transcendentals=0)
    north_shape = (3, QUADS, ROWS, COLS)
    south_shape = (2, QUADS, ROWS, COLS)
    one_shape = (1, QUADS, ROWS, COLS)
    lon_scr = pltpu.VMEM((2, 2, ROWS, HALF), F32)
    fold_scr = pltpu.VMEM((20, ROWS, COLS), F32)

    g1, slots1, north1, south1, lonc = pl.pallas_call(
        first_kernel,
        grid=grid,
        in_specs=[whole(field), vspec] + [whole(field)] * 4 + [whole((ROWS, COLS))],
        out_specs=[whole(field), whole(slot_shape), whole(north_shape), whole(south_shape),
                   whole((2, ROWS, COLS))],
        out_shape=[shaped(field, F32), shaped(slot_shape, BF16), shaped(north_shape, BF16),
                   shaped(south_shape, BF16), shaped((2, ROWS, COLS), BF16)],
        scratch_shapes=[pltpu.VMEM(field, F32), fold_scr, lon_scr, lon_scr],
        compiler_params=params,
        cost_estimate=cost,
        name="vertical_first",
    )(lam, inverse, *coefs, depth)

    up = [(i, (i + 1) % lats) for i in range(lats)]
    down = [(i, (i - 1) % lats) for i in range(lats)]

    def exchange(north, south, slots):
        return (lax.ppermute(north, "lat", up), lax.ppermute(south, "lat", down),
                lax.all_to_all(slots, "lon", 0, 0, tiled=True))

    smem = pl.BlockSpec(memory_space=pltpu.SMEM)
    in_north1, in_south1, in_slots1 = exchange(north1, south1, slots1)
    relayed1 = pl.pallas_call(
        relay_kernel,
        in_specs=[smem, whole(slot_shape), whole((2, ROWS, COLS))],
        out_specs=whole(slot_shape),
        out_shape=shaped(slot_shape, BF16),
        name="relay_first",
    )(fold_block, in_slots1, lonc)
    fold1 = lax.all_to_all(relayed1, "lon", 0, 0, tiled=True)

    g2, slots2, north2, south2 = pl.pallas_call(
        second_kernel,
        grid=grid,
        in_specs=[whole(field), vspec] + [whole(field)] * 4
        + [whole((ROWS, COLS)), whole(slot_shape), whole(slot_shape), whole(north_shape), whole(south_shape)],
        out_specs=[whole(field), whole(slot_shape), whole(one_shape), whole(one_shape)],
        out_shape=[shaped(field, F32), shaped(slot_shape, BF16), shaped(one_shape, BF16),
                   shaped(one_shape, BF16)],
        scratch_shapes=[pltpu.VMEM(field, F32), fold_scr, lon_scr],
        compiler_params=params,
        cost_estimate=cost,
        name="horizontal_vertical",
    )(g1, inverse, *coefs, depth, in_slots1, fold1, in_north1, in_south1)

    in_north2, in_south2, in_slots2 = exchange(north2, south2, slots2)
    relayed2 = pl.pallas_call(
        plain_relay,
        in_specs=[smem, whole(slot_shape)],
        out_specs=whole(slot_shape),
        out_shape=shaped(slot_shape, BF16),
        name="relay_second",
    )(fold_block, in_slots2)
    fold2 = lax.all_to_all(relayed2, "lon", 0, 0, tiled=True)

    return pl.pallas_call(
        third_kernel,
        in_specs=[whole(field)] * 5
        + [whole((ROWS, COLS)), whole(slot_shape), whole(slot_shape), whole(slot_shape), whole(one_shape),
           whole(one_shape), whole(north_shape), whole(south_shape)],
        out_specs=whole(field),
        out_shape=shaped(field, F32),
        compiler_params=params,
        name="horizontal_last",
    )(g2, *coefs, depth, in_slots2, fold1, fold2, in_north2, in_south2, in_north1, in_south1)


def solution(mesh):
    return jax.shard_map(
        per_device,
        mesh=mesh,
        in_specs=(
            P(None, "lat", "lon"),
            P(None, None, "lat", "lon"),
            P(None, "lat", "lon"),
            P(None, "lat", "lon"),
            P(None, "lat", "lon"),
            P(None, "lat", "lon"),
            P("lat", "lon"),
            P(),
        ),
        out_specs=P(None, "lat", "lon"),
        check_vma=False,
    )
```

```python
import jax
import jax.numpy as jnp
from jax import lax
from jax.experimental import pallas as pl
from jax.experimental.pallas import tpu as pltpu
from jax.sharding import PartitionSpec as P

F32 = jnp.float32
BF16 = jnp.bfloat16
LEV = 75
ROWS = 8
COLS = 256
HALF = 128
QUADS = 19
FULL_QUADS = 18
AHEAD = 4
HELD = 0
TAIL = LEV - 4 * FULL_QUADS
MIX_LANE = 22


def lane_ids():
    return lax.broadcasted_iota(jnp.int32, (ROWS, HALF), 1)


def row_ids():
    return lax.broadcasted_iota(jnp.int32, (ROWS, HALF), 0)


def turn(tile, shift, axis):
    size = tile.shape[axis]
    if isinstance(shift, int):
        shift = shift % size
        if shift == 0:
            return tile
    return pltpu.roll(tile, shift, axis)


def halves(value):
    return [value[:, :HALF], value[:, HALF:]]


def for_quads(body):
    def step(quad, carry):
        body(quad, 4)
        return carry

    lax.fori_loop(0, FULL_QUADS, step, 0)
    body(FULL_QUADS, TAIL)


def vertical_sums(inverse_ref, weighted_ref, first_level, count):
    group = 15

    def some_levels(step, sums):
        sums = list(sums)
        for offset in range(group):
            k = step * group + offset
            weight = weighted_ref[k]
            for jj in range(count):
                sums[jj] = sums[jj] + inverse_ref[k, first_level + jj].astype(F32) * weight
        return tuple(sums)

    zero = jnp.zeros((ROWS, COLS), F32)
    return lax.fori_loop(0, LEV // group, some_levels, (zero,) * count)


def place_lanes(acc_ref, side, j, tile, from_lane):
    spot = lax.rem(j, 64)
    which = j // 64
    rolled = pltpu.roll(tile, lax.rem(2 * spot + (2 * HALF - from_lane), HALF), 1)
    keep = (lane_ids() // 2) == spot
    acc_ref[side, which] = jnp.where(keep, rolled, acc_ref[side, which])


def place_mix(acc_ref, side, j, tile):
    lane = MIX_LANE + j
    rolled = pltpu.roll(tile, lax.rem(lane + 1, HALF), 1)
    acc_ref[side, 1] = jnp.where(lane_ids() == lane, rolled, acc_ref[side, 1])


def pack_quad(quad, gs, sn_ref, mn_ref, se_ref, me_ref, north_ref, south_ref,
              fold_scr, lon_scr, lonc_scr, with_coefs):
    row = row_ids()
    count = len(gs)
    is_top = lax.axis_index("lat") == lax.axis_size("lat") - 1

    def gathered(tiles_of, shift):
        for c in range(2):
            value = jnp.zeros((ROWS, HALF), F32)
            for l in range(count):
                moved = turn(tiles_of(l)[c], 2 * l - shift, 0)
                value = jnp.where((row // 2) == l, moved, value)
            yield slice(c * HALF, (c + 1) * HALF), value

    def level_of(ref):
        return lambda l: halves(ref[quad * 4 + l].astype(F32))

    for cols, value in gathered(lambda l: halves(gs[l]), 0):
        south_ref[0, quad, :, cols] = value.astype(BF16)
    if with_coefs:
        for cols, value in gathered(level_of(sn_ref), 0):
            south_ref[1, quad, :, cols] = value.astype(BF16)

    @pl.when(jnp.logical_not(is_top))
    def _():
        for cols, value in gathered(lambda l: halves(gs[l]), 6):
            north_ref[0, quad, :, cols] = value.astype(BF16)
        if with_coefs:
            for cols, value in gathered(level_of(sn_ref), 6):
                north_ref[1, quad, :, cols] = value.astype(BF16)
            for cols, value in gathered(level_of(mn_ref), 6):
                north_ref[2, quad, :, cols] = value.astype(BF16)

    @pl.when(is_top)
    def _():
        def ghosts(l):
            g = halves(gs[l])
            s = level_of(sn_ref)(l)
            m = level_of(mn_ref)(l)
            result = []
            for c in range(2):
                slope = s[c] * (1.0 / 12.0)
                direct = g[c] * (m[c] - 7.0 * slope)
                inner = (g[c] - turn(g[c], -1, 0)) * slope
                result.append(jnp.where(row == 7, direct + turn(inner, 1, 0), turn(slope * g[c], -1, 0)))
            return result

        for cols, value in gathered(ghosts, 6):
            fold_scr[quad, :, cols] = value

    for l in range(count):
        j = quad * 4 + l
        g = halves(gs[l])
        place_lanes(lon_scr, 0, j, g[1], 126)
        place_lanes(lon_scr, 1, j, g[0], 0)
        if with_coefs:
            se = level_of(se_ref)(l)
            me = level_of(me_ref)(l)
            place_lanes(lonc_scr, 0, j, se[1], 126)
            place_lanes(lonc_scr, 1, j, se[0], 0)
            place_mix(lonc_scr, 0, j, me[1])


def fill_slots(slots_ref, fold_scr, lon_scr, lonc_scr, with_coefs):
    is_top = lax.axis_index("lat") == lax.axis_size("lat") - 1

    @pl.when(is_top)
    def _():
        r = lax.broadcasted_iota(jnp.int32, (COLS, COLS), 0)
        q = lax.broadcasted_iota(jnp.int32, (COLS, COLS), 1)
        mirror = (r + q == COLS - 1).astype(F32).astype(BF16)
        flat = fold_scr[...].reshape(20 * ROWS, COLS).astype(BF16)
        fold_scr[...] = jnp.dot(flat, mirror, preferred_element_type=F32).reshape(20, ROWS, COLS)

    count = lax.axis_size("lon")
    me_lon = lax.axis_index("lon")
    east = lax.rem(me_lon + 1, count)
    west = lax.rem(me_lon + count - 1, count)

    def wide(ref, side):
        return jnp.concatenate([ref[side, 0], ref[side, 1]], axis=1)

    to_east = wide(lon_scr, 0)
    to_west = wide(lon_scr, 1)
    if with_coefs:
        to_east = jnp.concatenate([to_east, wide(lonc_scr, 0)], axis=0)
        to_west = jnp.concatenate([to_west, wide(lonc_scr, 1)], axis=0)
    for i in range(count):
        rim = jnp.where(i == east, to_east, to_west)
        slots_ref[i] = jnp.concatenate([fold_scr[min(i, QUADS)], rim], axis=0).astype(BF16)


def transposed_h(g_ref, se_ref, me_ref, sn_ref, mn_ref, depth_ref, slots_ref, coef_slots_ref,
                 north_ref, south_ref, north_c_ref, south_c_ref, out_ref):
    row = row_ids()
    lane = lane_ids()
    count = lax.axis_size("lon")
    me_lon = lax.axis_index("lon")
    east = lax.rem(me_lon + 1, count)
    west = lax.rem(me_lon + count - 1, count)
    lat = lax.axis_index("lat")
    has_south = lat > 0
    has_north = lat < lax.axis_size("lat") - 1

    def pick(ref, which, part):
        return halves(ref[which].astype(F32)[part * ROWS:(part + 1) * ROWS])

    def kept(value, condition):
        return halves(jnp.where(condition, value.astype(F32), 0.0))

    gw, ge = pick(slots_ref, west, 1), pick(slots_ref, east, 1)
    cw, ce = pick(coef_slots_ref, west, 2), pick(coef_slots_ref, east, 2)

    def quad_body(quad, levels):
        g_n = kept(north_ref[0, quad], has_south)
        s_n = kept(north_c_ref[1, quad], has_south)
        m_n = kept(north_c_ref[2, quad], has_south)
        g_s = kept(south_ref[0, quad], has_north)
        s_s = kept(south_c_ref[1, quad], has_north)
        for l in range(levels):
            j = quad * 4 + l
            depth = halves(depth_ref[...])
            g = halves(g_ref[j])
            se = halves(se_ref[j].astype(F32))
            me = halves(me_ref[j].astype(F32))
            sn = halves(sn_ref[j].astype(F32))
            mn = halves(mn_ref[j].astype(F32))
            first = j < 64
            at = 2 * lax.rem(j, 64)
            back = lax.rem(HALF - at, HALF)
            fore = lax.rem(2 * HALF - 2 - at, HALF)
            g_rim = jnp.where(
                lane < 64,
                pltpu.roll(jnp.where(first, ge[0], ge[1]), back, 1),
                pltpu.roll(jnp.where(first, gw[0], gw[1]), fore, 1),
            )
            s_rim = jnp.where(
                lane < 64,
                pltpu.roll(jnp.where(first, ce[0], ce[1]), back, 1),
                pltpu.roll(jnp.where(first, cw[0], cw[1]), fore, 1),
            )
            m_rim = pltpu.roll(cw[1], lax.rem(2 * HALF - 1 - MIX_LANE - j, HALF), 1)
            tiles = [g[0], g[1], g_rim]
            ahead = [turn(jnp.where(lane == 0, tiles[(c + 1) % 3], tiles[c]), -1, 1) for c in range(3)]
            jump = [ahead[c] - tiles[c] for c in range(3)]
            slope = [x * (1.0 / 12.0) for x in (se[0], se[1], s_rim)]
            mixes = [me[0], me[1], m_rim]
            far = [-slope[c] * jump[c] for c in range(3)]
            high = [(7.0 * slope[c] - mixes[c]) * jump[c] for c in range(3)]
            total = []
            for c in range(2):
                before = (c + 2) % 3
                after = c + 1
                value = g[c] + (7.0 * slope[c] + mixes[c]) * jump[c]
                value = value + turn(jnp.where(lane == 127, high[before], high[c]), 1, 1)
                value = value + turn(jnp.where(lane == 0, far[after], far[c]), -1, 1)
                value = value + turn(jnp.where(lane >= 126, far[before], far[c]), 2, 1)
                total.append(value)
            for c in range(2):
                rim = jnp.where(row < 4, turn(g_s[c], -2 * l, 0), turn(g_n[c], 6 - 2 * l, 0))
                s_r = jnp.where(row < 4, turn(s_s[c], -2 * l, 0), turn(s_n[c], 6 - 2 * l, 0)) * (1.0 / 12.0)
                m_r = turn(m_n[c], 6 - 2 * l, 0)
                d = turn(jnp.where(row == 0, rim, g[c]), -1, 0) - g[c]
                d_r = turn(jnp.where(row == 0, g[c], rim), -1, 0) - rim
                sl = sn[c] * (1.0 / 12.0)
                hi = (7.0 * sl - mn[c]) * d
                hi_r = (7.0 * s_r - m_r) * d_r
                fa = -sl * d
                fa_r = -s_r * d_r
                value = total[c] + (7.0 * sl + mn[c]) * d
                value = value + turn(jnp.where(row == 7, hi_r, hi), 1, 0)
                value = value + turn(jnp.where(row == 0, fa_r, fa), -1, 0)
                value = value + turn(jnp.where(row >= 6, fa_r, fa), 2, 0)
                out_ref[j, :, c * HALF:(c + 1) * HALF] = jnp.where(depth[c] > j, value, 0.0)

    for_quads(quad_body)


def add_fold(pre_ref, fold_ref, depth_ref, put):
    row = row_ids()
    depth = halves(depth_ref[...])
    on_top = lax.axis_index("lat") == lax.axis_size("lat") - 1

    def quad_body(quad, levels):
        fold = halves(fold_ref[quad].astype(F32))
        for l in range(levels):
            j = quad * 4 + l
            for c in range(2):
                cols = slice(c * HALF, (c + 1) * HALF)
                use = ((row == 5) | (row == 6)) & (depth[c] > j) & on_top
                put(j, cols, pre_ref[j, :, cols] + jnp.where(use, turn(fold[c], 5 - 2 * l, 0), 0.0))

    for_quads(quad_body)


def first_kernel(lam_hbm, inv_hbm, se_hbm, me_hbm, sn_hbm, mn_hbm, depth_hbm,
                 g_ref, slots_ref, north_ref, south_ref,
                 lam, inverse, se, me, sn, mn, depth_ref, fold_scr, lon_scr, lonc_scr, small_sem, sem):
    small = [pltpu.make_async_copy(src, dst, small_sem.at[i])
             for i, (src, dst) in enumerate([(depth_hbm, depth_ref), (lam_hbm, lam), (sn_hbm, sn),
                                             (mn_hbm, mn), (se_hbm, se), (me_hbm, me)])]

    def levels_copy(quad, count):
        part = pl.ds(quad * 4, count)
        return pltpu.make_async_copy(inv_hbm.at[:, part], inverse.at[:, part], sem.at[quad])

    small[0].start()
    small[1].start()
    levels_copy(0, 4).start()
    levels_copy(1, 4).start()
    for copy in small[2:]:
        copy.start()
    for quad in range(2, AHEAD):
        levels_copy(quad, 4).start()
    small[0].wait()
    small[1].wait()
    depth = depth_ref[...]

    def mask(k, carry):
        lam[k] = jnp.where(depth > k, lam[k], 0.0)
        return carry

    lax.fori_loop(0, LEV, mask, 0, unroll=5)
    for copy in small[2:]:
        copy.wait()

    def quad_body(quad, count):
        if count == 4:
            @pl.when(quad + AHEAD < FULL_QUADS)
            def _():
                levels_copy(quad + AHEAD, 4).start()

            @pl.when(quad + AHEAD == FULL_QUADS)
            def _():
                levels_copy(FULL_QUADS, TAIL).start()

        levels_copy(quad, count).wait()
        sums = vertical_sums(inverse, lam, quad * 4, count)
        gs = [jnp.where(depth > quad * 4 + l, sums[l], 0.0) for l in range(count)]
        for l in range(count):
            g_ref[quad * 4 + l] = gs[l]
        pack_quad(quad, gs, sn, mn, se, me, north_ref, south_ref, fold_scr, lon_scr, lonc_scr, True)

    for_quads(quad_body)
    fill_slots(slots_ref, fold_scr, lon_scr, lonc_scr, True)


def second_kernel(pre_ref, fold_ref, inv_hbm, sn_ref, mn_ref, depth_ref,
                  g_ref, slots_ref, north_ref, south_ref, lam, rest, fold_scr, lon_scr, sem):
    def levels_copy(quad, count):
        return pltpu.make_async_copy(inv_hbm.at[:, pl.ds(quad * 4, count)],
                                     rest.at[:, pl.ds((quad - HELD) * 4, count)], sem.at[quad - HELD])

    for quad in range(HELD, HELD + AHEAD):
        levels_copy(quad, 4).start()

    def put(j, cols, value):
        lam[j, :, cols] = value

    add_fold(pre_ref, fold_ref, depth_ref, put)
    depth = depth_ref[...]

    def quad_body(quad, count, source_ref, first_level):
        sums = vertical_sums(source_ref, lam, first_level, count)
        gs = [jnp.where(depth > quad * 4 + l, sums[l], 0.0) for l in range(count)]
        for l in range(count):
            g_ref[quad * 4 + l] = gs[l]
        pack_quad(quad, gs, sn_ref, mn_ref, None, None, north_ref, south_ref, fold_scr, lon_scr, None, False)

    def rest_quad(quad, carry):
        @pl.when(quad + AHEAD < FULL_QUADS)
        def _():
            levels_copy(quad + AHEAD, 4).start()

        @pl.when(quad + AHEAD == FULL_QUADS)
        def _():
            levels_copy(FULL_QUADS, TAIL).start()

        levels_copy(quad, 4).wait()
        quad_body(quad, 4, rest, (quad - HELD) * 4)
        return carry

    lax.fori_loop(HELD, FULL_QUADS, rest_quad, 0)
    levels_copy(FULL_QUADS, TAIL).wait()
    quad_body(FULL_QUADS, TAIL, rest, (FULL_QUADS - HELD) * 4)
    fill_slots(slots_ref, fold_scr, lon_scr, None, False)


def last_kernel(pre_ref, fold_ref, depth_ref, out_hbm, total, sem):
    def put(j, cols, value):
        total[j, :, cols] = value

    add_fold(pre_ref, fold_ref, depth_ref, put)
    copy = pltpu.make_async_copy(total, out_hbm, sem)
    copy.start()
    copy.wait()


def relay_kernel(fold_ref, in_ref, *rest):
    out_ref = rest[-1]
    for d in range(out_ref.shape[0]):
        out_ref[d] = in_ref[fold_ref[d]].astype(F32)[:ROWS].astype(BF16)


def shaped(shape, dtype):
    return jax.ShapeDtypeStruct(shape, dtype)


def per_device(lam, inverse, se, me, sn, mn, depth, fold_block):
    field = (LEV, ROWS, COLS)
    count = lax.axis_size("lon")
    lats = lax.axis_size("lat")
    vmem = pl.BlockSpec(memory_space=pltpu.VMEM)
    hbm = pl.BlockSpec(memory_space=pltpu.HBM)
    smem = pl.BlockSpec(memory_space=pltpu.SMEM)
    anywhere = pl.BlockSpec(memory_space=pl.ANY)
    coefs = [se, me, sn, mn]
    lon_scr = pltpu.VMEM((2, 2, ROWS, HALF), F32)
    fold_scr = pltpu.VMEM((20, ROWS, COLS), F32)
    bf_field = pltpu.VMEM(field, BF16)
    work = 2 * LEV * LEV * ROWS * COLS
    mib = 1024 * 1024
    beside = pl.CostEstimate(flops=work, bytes_accessed=2 * LEV * LEV * ROWS * COLS, transcendentals=0)

    def rims(north, south, rows):
        return [shaped((count, rows, COLS), BF16), shaped((north, QUADS, ROWS, COLS), BF16),
                shaped((south, QUADS, ROWS, COLS), BF16)]

    g1, slots1, north1, south1 = pl.pallas_call(
        first_kernel,
        in_specs=[hbm] * 7,
        out_specs=[vmem] * 4,
        out_shape=[shaped(field, F32)] + rims(3, 2, 3 * ROWS),
        scratch_shapes=[pltpu.VMEM(field, F32), pltpu.VMEM((LEV,) + field, BF16)] + [bf_field] * 4
        + [pltpu.VMEM((ROWS, COLS), jnp.int32), fold_scr, lon_scr, lon_scr,
           pltpu.SemaphoreType.DMA((6,)), pltpu.SemaphoreType.DMA((QUADS,))],
        compiler_params=pltpu.CompilerParams(vmem_limit_bytes=62 * mib),
        cost_estimate=pl.CostEstimate(flops=work, bytes_accessed=2 * LEV * LEV * ROWS * COLS, transcendentals=0),
        name="vertical_first",
    )(lam, inverse, *coefs, depth)

    up = [(i, (i + 1) % lats) for i in range(lats)]
    down = [(i, (i - 1) % lats) for i in range(lats)]

    def fold_route(slots, north, south, order):
        north = lax.ppermute(north, "lat", up)
        south = lax.ppermute(south, "lat", down)
        slots = lax.all_to_all(slots, "lon", 0, 0, tiled=True)
        relayed = pl.pallas_call(
            relay_kernel,
            in_specs=[smem, vmem] + [anywhere] * (2 * order),
            out_specs=vmem,
            out_shape=shaped((count, ROWS, COLS), BF16),
            compiler_params=pltpu.CompilerParams(vmem_limit_bytes=4 * mib),
            cost_estimate=beside,
            name="relay",
        )(fold_block, slots, *((north, south) if order else ()))
        return slots, north, south, lax.all_to_all(relayed, "lon", 0, 0, tiled=True)

    params = pltpu.CompilerParams(vmem_limit_bytes=4 * mib)
    slots1, north1, south1, fold1 = fold_route(slots1, north1, south1, False)
    pre1 = pl.pallas_call(
        transposed_h,
        in_specs=[vmem] * 12,
        out_specs=vmem,
        out_shape=shaped(field, F32),
        compiler_params=params,
        cost_estimate=beside,
        name="horizontal_first",
    )(g1, *coefs, depth, slots1, slots1, north1, south1, north1, south1)

    g2, slots2, north2, south2 = pl.pallas_call(
        second_kernel,
        in_specs=[vmem] * 2 + [hbm] + [vmem] * 3,
        out_specs=[vmem] * 4,
        out_shape=[shaped(field, F32)] + rims(1, 1, 2 * ROWS),
        scratch_shapes=[pltpu.VMEM(field, F32), pltpu.VMEM((LEV, LEV - 4 * HELD, ROWS, COLS), BF16), fold_scr, lon_scr,
                        pltpu.SemaphoreType.DMA((QUADS - HELD,))],
        compiler_params=pltpu.CompilerParams(vmem_limit_bytes=44 * mib),
        cost_estimate=pl.CostEstimate(flops=work, bytes_accessed=8 * LEV * ROWS * COLS, transcendentals=0),
        name="vertical_second",
    )(pre1, fold1, inverse, sn, mn, depth)

    slots2, north2, south2, fold2 = fold_route(slots2, north2, south2, True)
    pre2 = pl.pallas_call(
        transposed_h,
        in_specs=[vmem] * 12,
        out_specs=vmem,
        out_shape=shaped(field, F32),
        compiler_params=params,
        cost_estimate=beside,
        name="horizontal_second",
    )(g2, *coefs, depth, slots2, slots1, north2, south2, north1, south1)

    return pl.pallas_call(
        last_kernel,
        in_specs=[vmem] * 3,
        out_specs=hbm,
        out_shape=shaped(field, F32),
        scratch_shapes=[pltpu.VMEM(field, F32), pltpu.SemaphoreType.DMA],
        compiler_params=pltpu.CompilerParams(vmem_limit_bytes=4 * mib),
        name="add_fold",
    )(pre2, fold2, depth)


def solution(mesh):
    return jax.shard_map(
        per_device,
        mesh=mesh,
        in_specs=(
            P(None, "lat", "lon"),
            P(None, None, "lat", "lon"),
            P(None, "lat", "lon"),
            P(None, "lat", "lon"),
            P(None, "lat", "lon"),
            P(None, "lat", "lon"),
            P("lat", "lon"),
            P(),
        ),
        out_specs=P(None, "lat", "lon"),
        check_vma=False,
    )
```

```python
import jax
import jax.numpy as jnp
from jax import lax
from jax.experimental import pallas as pl
from jax.experimental.pallas import tpu as pltpu
from jax.sharding import PartitionSpec as P

F32 = jnp.float32
BF16 = jnp.bfloat16
LEV = 75
ROWS = 8
COLS = 256
HALF = 128
QUADS = 19
FULL_QUADS = 18
AHEAD = 4
TOGETHER = 3
NEAR = 8
EXT = LEV + 3
TAIL = LEV - 4 * FULL_QUADS


def lane_ids():
    return lax.broadcasted_iota(jnp.int32, (ROWS, HALF), 1)


def row_ids():
    return lax.broadcasted_iota(jnp.int32, (ROWS, HALF), 0)


def turn(tile, shift, axis):
    size = tile.shape[axis]
    if isinstance(shift, int):
        shift = shift % size
        if shift == 0:
            return tile
    return pltpu.roll(tile, shift, axis)


def halves(value):
    return [value[:, :HALF], value[:, HALF:]]


def for_quads(body):
    def step(quad, carry):
        body(quad, 4)
        return carry

    lax.fori_loop(0, FULL_QUADS, step, 0)
    body(FULL_QUADS, TAIL)


def vertical_sums(inverse_ref, weighted_ref, first_level, count):
    sums = [None] * count
    for k in range(LEV):
        weight = weighted_ref[k]
        for jj in range(count):
            term = inverse_ref[k, first_level + jj].astype(F32) * weight
            sums[jj] = term if k == 0 else sums[jj] + term
    return sums


def sum_quads(inverse_ref, weighted_ref, depth, g_ref, levels_copy, pack):
    def sum_one(quad, count):
        sums = vertical_sums(inverse_ref, weighted_ref, quad * 4, count)
        for l in range(count):
            g_ref[quad * 4 + l] = jnp.where(depth > quad * 4 + l, sums[l], 0.0)

    def step(quad, carry):
        start_ahead(quad, levels_copy)
        levels_copy(quad, 4).wait()
        pack(jnp.maximum(quad - 1, 0), 4, lambda: sum_one(quad, 4))
        return carry

    lax.fori_loop(0, FULL_QUADS, step, 0)
    levels_copy(FULL_QUADS, TAIL).wait()
    pack(FULL_QUADS - 1, 4, lambda: sum_one(FULL_QUADS, TAIL))
    pack(FULL_QUADS, TAIL, None)


def place_lanes(acc_ref, side, quad, tiles, from_lane, ahead):
    which = quad // 16
    first = lax.rem(quad, 16) * 4
    lane = lane_ids()
    total = acc_ref[side, which]
    for l, tile in enumerate(tiles):
        spot = first + l
        rolled = pltpu.roll(tile, lax.rem(2 * spot + ahead + (2 * HALF - from_lane), HALF), 1)
        total = jnp.where((lane // 2) == lax.rem(spot + ahead // 2, 64), rolled, total)
    acc_ref[side, which] = total


def pack_quad(quad, count, g_ref, sn_ref, mn_ref, se_ref, me_ref, north_ref, south_ref,
              fold_scr, lon_scr, lonc_scr, with_coefs, beside=None):
    row = row_ids()
    gs = [g_ref[quad * 4 + l] for l in range(count)]
    is_top = lax.axis_index("lat") == lax.axis_size("lat") - 1

    def gathered(tiles_of, shift, ahead=0):
        for c in range(2):
            value = jnp.zeros((ROWS, HALF), F32)
            for l in range(count):
                moved = turn(tiles_of(l)[c], 2 * l + 2 * ahead - shift, 0)
                value = jnp.where((row // 2) == (l + ahead) % 4, moved, value)
            yield slice(c * HALF, (c + 1) * HALF), value

    def level_of(ref):
        return lambda l: halves(ref[quad * 4 + l].astype(F32))

    for cols, value in gathered(lambda l: halves(gs[l]), 0, 1):
        south_ref[0, quad, :, cols] = value.astype(BF16)
    if with_coefs:
        for cols, value in gathered(level_of(sn_ref), 0, 1):
            south_ref[1, quad, :, cols] = value.astype(BF16)

    place_lanes(lon_scr, 0, quad, [g[:, HALF:] for g in gs], 126, 0)
    place_lanes(lon_scr, 1, quad, [g[:, :HALF] for g in gs], 0, 2)
    if with_coefs:
        se = [level_of(se_ref)(l) for l in range(count)]
        me = [level_of(me_ref)(l)[1] for l in range(count)]
        place_lanes(lonc_scr, 0, quad, [tile[1] for tile in se], 126, 0)
        place_lanes(lonc_scr, 2, quad, me, 126, 0)
        place_lanes(lonc_scr, 1, quad, [tile[0] for tile in se], 0, 2)
    if beside is not None:
        beside()

    @pl.when(jnp.logical_not(is_top))
    def _():
        for cols, value in gathered(lambda l: halves(gs[l]), 6):
            north_ref[0, quad, :, cols] = value.astype(BF16)
        if with_coefs:
            for cols, value in gathered(level_of(sn_ref), 6):
                north_ref[1, quad, :, cols] = value.astype(BF16)
            for cols, value in gathered(level_of(mn_ref), 6):
                north_ref[2, quad, :, cols] = value.astype(BF16)

    @pl.when(is_top)
    def _():
        def ghosts(l):
            g = halves(gs[l])
            s = level_of(sn_ref)(l)
            m = level_of(mn_ref)(l)
            result = []
            for c in range(2):
                slope = s[c] * (1.0 / 12.0)
                direct = g[c] * (m[c] - 7.0 * slope)
                inner = (g[c] - turn(g[c], -1, 0)) * slope
                result.append(jnp.where(row == 7, direct + turn(inner, 1, 0), turn(slope * g[c], -1, 0)))
            return result

        for cols, value in gathered(ghosts, 6):
            fold_scr[quad, :, cols] = value


def fill_sends(slots_hbm, fold_scr, lon_scr, lonc_scr, flipped_scr, rim_scr, slot_sem, rim_sem):
    near = lax.axis_index("near")
    is_top = lax.axis_index("lat") == lax.axis_size("lat") - 1
    parts = rim_scr.shape[1]
    folds = [pltpu.make_async_copy(flipped_scr, slots_hbm.at[i, pl.ds(0, QUADS)], slot_sem.at[i])
             for i in range(NEAR)]
    rims = [pltpu.make_async_copy(rim_scr.at[side], slots_hbm.at[slot, pl.ds(QUADS, parts)], rim_sem.at[side])
            for side, slot in enumerate((lax.rem(near + 1, NEAR), lax.rem(near + NEAR - 1, NEAR)))]
    for side in range(2):
        for part, (ref, which) in enumerate(((lon_scr, side), (lonc_scr, side), (lonc_scr, 2))[:parts]):
            rim_scr[side, part] = jnp.concatenate([ref[which, 0], ref[which, 1]], axis=1).astype(BF16)
        rims[side].start()

    @pl.when(is_top)
    def _():
        r = lax.broadcasted_iota(jnp.int32, (COLS, COLS), 0)
        q = lax.broadcasted_iota(jnp.int32, (COLS, COLS), 1)
        mirror = (r + q == COLS - 1).astype(F32).astype(BF16)
        flat = fold_scr[...].reshape(20 * ROWS, COLS).astype(BF16)
        flipped = jnp.dot(flat, mirror, preferred_element_type=F32).reshape(20, ROWS, COLS)
        flipped_scr[...] = flipped[:QUADS].astype(BF16)
        for copy in folds:
            copy.start()
        for copy in folds:
            copy.wait()

    for copy in rims:
        copy.wait()


def transposed_h(g_ref, se_ref, me_ref, sn_ref, mn_ref, depth_ref, north_ref, south_ref,
                 north_c_ref, south_c_ref, out_ref):
    row = row_ids()
    lane = lane_ids()
    lat = lax.axis_index("lat")
    has_south = lat > 0
    has_north = lat < lax.axis_size("lat") - 1

    def kept(value, condition):
        return halves(jnp.where(condition, value.astype(F32), 0.0))

    def quad_body(quad, levels):
        g_n = kept(north_ref[0, quad], has_south)
        s_n = kept(north_c_ref[1, quad], has_south)
        m_n = kept(north_c_ref[2, quad], has_south)
        g_s = kept(south_ref[0, quad], has_north)
        s_s = kept(south_c_ref[1, quad], has_north)
        ready = []
        for l in range(levels):
            j = quad * 4 + l
            depth = halves(depth_ref[...])
            g = halves(g_ref[j])
            se = halves(se_ref[j].astype(F32))
            me = halves(me_ref[j].astype(F32))
            sn = halves(sn_ref[j].astype(F32))
            mn = halves(mn_ref[j].astype(F32))
            nothing = jnp.zeros((ROWS, HALF), F32)
            tiles = [g[0], g[1], nothing]
            jump = [turn(jnp.where(lane == 0, tiles[c + 1], tiles[c]), -1, 1) - tiles[c] for c in range(2)]
            speeds = [se[0], se[1]]
            mixes = [me[0], me[1]]
            far = [speeds[c] * (jump[c] * (1.0 / 12.0)) for c in range(2)] + [nothing]
            seven = [7.0 * far[c] for c in range(2)]
            mixed = [mixes[c] * jump[c] for c in range(2)]
            high = [seven[c] - mixed[c] for c in range(2)] + [nothing]
            total = []
            for c in range(2):
                before = (c + 2) % 3
                after = c + 1
                value = g[c] + seven[c] + mixed[c]
                value = value + turn(jnp.where(lane == 127, high[before], high[c]), 1, 1)
                value = value - turn(jnp.where(lane == 0, far[after], far[c]), -1, 1)
                value = value - turn(jnp.where(lane >= 126, far[before], far[c]), 2, 1)
                total.append(value)
            for c in range(2):
                pair = (row // 2) == l
                rim = turn(jnp.where(pair, g_n[c], g_s[c]), 6 - 2 * l, 0)
                s_r = turn(jnp.where(pair, s_n[c], s_s[c]), 6 - 2 * l, 0)
                m_r = turn(m_n[c], 6 - 2 * l, 0)
                d = turn(jnp.where(row == 0, rim, g[c]), -1, 0) - g[c]
                d_r = turn(jnp.where(row == 0, g[c], rim), -1, 0) - rim
                fa = sn[c] * (d * (1.0 / 12.0))
                fa_r = s_r * (d_r * (1.0 / 12.0))
                seven_y = 7.0 * fa
                mixed_y = mn[c] * d
                hi = seven_y - mixed_y
                hi_r = 7.0 * fa_r - m_r * d_r
                value = total[c] + seven_y + mixed_y
                value = value + turn(jnp.where(row == 7, hi_r, hi), 1, 0)
                value = value - turn(jnp.where(row == 0, fa_r, fa), -1, 0)
                value = value - turn(jnp.where(row >= 6, fa_r, fa), 2, 0)
                ready.append((j, c, jnp.where(depth[c] > j, value, 0.0)))
        for j, c, value in ready:
            out_ref[j, :, c * HALF:(c + 1) * HALF] = value

    for_quads(quad_body)
    for part in range(LEV, EXT):
        out_ref[part] = g_ref[part]


def lon_rims(near_ref, far1_ref, far3_ref, part):
    near = lax.axis_index("near")
    west = near_ref[lax.rem(near + NEAR - 1, NEAR), QUADS + part].astype(F32)
    east = near_ref[lax.rem(near + 1, NEAR), QUADS + part].astype(F32)
    west = jnp.where(near == 0, far1_ref[QUADS + part].astype(F32), west)
    east = jnp.where(near == NEAR - 1, far3_ref[QUADS + part].astype(F32), east)
    return west, east


def lon_edges(west_g, east_g, west_s, west_m, east_s, own_ref):
    lane = lane_ids()
    west_edge, east_edge = [], []
    even = lane % 2 == 0

    for w, e, own, w_s, w_m, e_s, o_s, o_m in zip(*map(halves, (
            west_g, east_g, own_ref[LEV], west_s, west_m, east_s, own_ref[LEV + 1], own_ref[LEV + 2]))):
        jump_w = jnp.where(even, turn(w, -1, 1), turn(own, -1, 1)) - w
        far_w = w_s * (jump_w * (1.0 / 12.0))
        high_w = 7.0 * far_w - w_m * jump_w
        west_edge.append(turn(jnp.where(even, turn(high_w, -1, 1) - far_w, -far_w), 2, 1))
        next_e = turn(e, -1, 1)
        far_e = e_s * ((next_e - e) * (1.0 / 12.0))
        far_o = o_s * (next_e * (1.0 / 12.0))
        east_edge.append(jnp.where(even, -turn(far_o, -1, 1), 7.0 * far_o + o_m * next_e - turn(far_e, -1, 1)))
    return west_edge, east_edge


def place_of(block):
    return block // NEAR, lax.rem(block, NEAR)


def add_fold(pre_ref, fold_ref, near_ref, far_refs, rim_c, depth_ref, put, after=None):
    row = row_ids()
    lane = lane_ids()
    west_g, east_g = lon_rims(near_ref, far_refs[0], far_refs[2], 0)
    west_edge, east_edge = lon_edges(west_g, east_g, *rim_c, pre_ref)
    depth = halves(depth_ref[...])
    on_top = lax.axis_index("lat") == lax.axis_size("lat") - 1
    fars = lax.axis_size("far")
    my_far = lax.axis_index("far")
    far, near = place_of(fold_ref[my_far * NEAR + lax.axis_index("near")])
    steps = lax.rem(my_far - far + fars, fars)

    def quad_values(quad, levels):
        fold = near_ref[near, quad].astype(F32)
        for step, ref in enumerate(far_refs):
            fold = jnp.where(steps == step + 1, ref[quad].astype(F32), fold)
        fold = halves(fold)
        ready = []
        for l in range(levels):
            j = quad * 4 + l
            first = j < 64
            spot = lax.rem(j, 64)
            edge = jnp.where((lane // 2) == spot, jnp.where(first, east_edge[0], east_edge[1]),
                             jnp.where(first, west_edge[0], west_edge[1]))
            edge = pltpu.roll(edge, lax.rem(2 * HALF - 2 - 2 * spot, HALF), 1)
            for c in range(2):
                cols = slice(c * HALF, (c + 1) * HALF)
                at_edge = lane < 2 if c == 0 else lane >= 126
                more = jnp.where(at_edge, edge, 0.0)
                more = more + jnp.where(((row == 5) | (row == 6)) & on_top, turn(fold[c], 5 - 2 * l, 0), 0.0)
                ready.append((j, cols, pre_ref[j, :, cols] + jnp.where(depth[c] > j, more, 0.0)))
        return ready

    def several(step, carry):
        ready = []
        for part in range(TOGETHER):
            ready += quad_values(step * TOGETHER + part, 4)
        for j, cols, value in ready:
            put(j, cols, value)
        if after is not None:
            after(step * TOGETHER + TOGETHER - 1)
        return carry

    lax.fori_loop(0, FULL_QUADS // TOGETHER, several, 0)
    for j, cols, value in quad_values(FULL_QUADS, TAIL):
        put(j, cols, value)
    if after is not None:
        after(FULL_QUADS)


def start_ahead(quad, levels_copy):
    @pl.when(quad + AHEAD < FULL_QUADS)
    def _():
        levels_copy(quad + AHEAD, 4).start()

    @pl.when(quad + AHEAD == FULL_QUADS)
    def _():
        levels_copy(FULL_QUADS, TAIL).start()


def first_kernel(lam_hbm, inv_hbm, se_hbm, me_hbm, sn_hbm, mn_hbm, depth_hbm,
                 g_ref, slots_hbm, north_ref, south_ref,
                 lam, inverse, se, me, sn, mn, depth_ref, fold_scr, lon_scr, lonc_scr,
                 flipped_scr, rim_scr, small_sem, sem, slot_sem, rim_sem):
    small = [pltpu.make_async_copy(src, dst, small_sem.at[i])
             for i, (src, dst) in enumerate([(depth_hbm, depth_ref), (lam_hbm, lam), (sn_hbm, sn),
                                             (mn_hbm, mn), (se_hbm, se), (me_hbm, me)])]

    def levels_copy(quad, count):
        part = pl.ds(quad * 4, count)
        return pltpu.make_async_copy(inv_hbm.at[:, part], inverse.at[:, part], sem.at[quad])

    small[0].start()
    small[1].start()
    levels_copy(0, 4).start()
    levels_copy(1, 4).start()
    for copy in small[2:]:
        copy.start()
    for quad in range(2, AHEAD):
        levels_copy(quad, 4).start()
    small[0].wait()
    small[1].wait()
    depth = depth_ref[...]

    def mask(k, carry):
        lam[k] = jnp.where(depth > k, lam[k], 0.0)
        return carry

    lax.fori_loop(0, LEV, mask, 0, unroll=5)
    for copy in small[2:]:
        copy.wait()

    def pack(quad, count, beside):
        pack_quad(quad, count, g_ref, sn, mn, se, me, north_ref, south_ref, fold_scr, lon_scr, lonc_scr, True, beside)

    sum_quads(inverse, lam, depth, g_ref, levels_copy, pack)
    for part, (ref, side) in enumerate(((lon_scr, 1), (lonc_scr, 0), (lonc_scr, 2))):
        g_ref[LEV + part] = jnp.concatenate([ref[side, 0], ref[side, 1]], axis=1)
    fill_sends(slots_hbm, fold_scr, lon_scr, lonc_scr, flipped_scr, rim_scr, slot_sem, rim_sem)


def second_kernel(pre_ref, fold_ref, near_ref, far1_ref, far2_ref, far3_ref,
                  inv_hbm, sn_ref, mn_ref, depth_ref,
                  g_ref, slots_hbm, north_ref, south_ref, rim_c_ref,
                  lam, inverse, fold_scr, lon_scr, flipped_scr, rim_scr, sem, slot_sem, rim_sem):
    def levels_copy(quad, count):
        part = pl.ds(quad * 4, count)
        return pltpu.make_async_copy(inv_hbm.at[:, part], inverse.at[:, part], sem.at[quad])

    for quad in range(AHEAD):
        levels_copy(quad, 4).start()

    def put(j, cols, value):
        lam[j, :, cols] = value

    west_s, east_s = lon_rims(near_ref, far1_ref, far3_ref, 1)
    west_m, _ = lon_rims(near_ref, far1_ref, far3_ref, 2)
    for part, tile in enumerate((west_s, west_m, east_s)):
        rim_c_ref[part] = tile
    add_fold(pre_ref, fold_ref, near_ref, (far1_ref, far2_ref, far3_ref), (west_s, west_m, east_s), depth_ref, put)
    depth = depth_ref[...]

    def pack(quad, count, beside):
        pack_quad(quad, count, g_ref, sn_ref, mn_ref, None, None, north_ref, south_ref, fold_scr, lon_scr, None, False,
                  beside)

    sum_quads(inverse, lam, depth, g_ref, levels_copy, pack)
    g_ref[LEV] = jnp.concatenate([lon_scr[1, 0], lon_scr[1, 1]], axis=1)
    for part in range(LEV + 1, EXT):
        g_ref[part] = pre_ref[part]
    fill_sends(slots_hbm, fold_scr, lon_scr, None, flipped_scr, rim_scr, slot_sem, rim_sem)


def last_kernel(pre_ref, fold_ref, near_ref, far1_ref, far2_ref, far3_ref,
                rim_c_ref, depth_ref, out_hbm, total, sem):
    copies = [pltpu.make_async_copy(total.at[pl.ds(start, size)], out_hbm.at[pl.ds(start, size)], sem.at[i])
              for i, (start, size) in enumerate(((0, 24), (24, 24), (48, 27)))]

    def put(j, cols, value):
        total[j, :, cols] = value

    def after(quad):
        for i, last in enumerate((5, 11, FULL_QUADS)):
            @pl.when(quad == last)
            def _(copy=copies[i]):
                copy.start()

    add_fold(pre_ref, fold_ref, near_ref, (far1_ref, far2_ref, far3_ref),
             [rim_c_ref[part] for part in range(3)], depth_ref, put, after)
    for copy in copies:
        copy.wait()


def relay_kernel(fold_ref, near_ref, *refs):
    fars = lax.axis_size("far")
    my_far = lax.axis_index("far")
    my_near = lax.axis_index("near")
    far1_ref, _, far3_ref = refs[-3:]
    for ref, slot in ((far1_ref, lax.rem(my_near + NEAR - 1, NEAR)), (far3_ref, lax.rem(my_near + 1, NEAR))):
        for part in range(QUADS, ref.shape[0]):
            ref[part] = near_ref[slot, part]

    @pl.when(lax.axis_index("lat") == lax.axis_size("lat") - 1)
    def _():
        for step, out_ref in enumerate(refs[-3:]):
            target = lax.rem(my_far + step + 1, fars)
            _, near = place_of(fold_ref[target * NEAR + my_near])
            for quad in range(QUADS):
                out_ref[quad] = near_ref[near, quad]


def shaped(shape, dtype):
    return jax.ShapeDtypeStruct(shape, dtype)


def per_device(lam, inverse, se, me, sn, mn, depth, fold_block):
    field = (LEV, ROWS, COLS)
    extended = (EXT, ROWS, COLS)
    lats = lax.axis_size("lat")
    count = lax.axis_size("far") * NEAR
    lon = ("far", "near")
    vmem = pl.BlockSpec(memory_space=pltpu.VMEM)
    hbm = pl.BlockSpec(memory_space=pltpu.HBM)
    smem = pl.BlockSpec(memory_space=pltpu.SMEM)
    coefs = [se, me, sn, mn]
    lon_scr = pltpu.VMEM((2, 2, ROWS, HALF), F32)
    fold_scr = pltpu.VMEM((20, ROWS, COLS), F32)
    inverse_scr = pltpu.VMEM((LEV,) + field, BF16)
    quad_sems = pltpu.SemaphoreType.DMA((QUADS,))
    slot_sems = [pltpu.SemaphoreType.DMA((NEAR,)), pltpu.SemaphoreType.DMA((2,))]
    work = 2 * LEV * LEV * ROWS * COLS
    mib = 1024 * 1024
    block = (QUADS, ROWS, COLS)

    def cost(bytes_accessed):
        return pl.CostEstimate(flops=work, bytes_accessed=bytes_accessed, transcendentals=0)

    def limit(size):
        return pltpu.CompilerParams(vmem_limit_bytes=size * mib)

    def sends(north, south, parts):
        return [shaped((NEAR, QUADS + parts, ROWS, COLS), BF16), shaped((north,) + block, BF16),
                shaped((south,) + block, BF16)]

    def staging(parts):
        return [pltpu.VMEM(block, BF16), pltpu.VMEM((2, parts, ROWS, COLS), BF16)]

    g1, *sent1 = pl.pallas_call(
        first_kernel,
        in_specs=[hbm] * 7,
        out_specs=[vmem, hbm, vmem, vmem],
        out_shape=[shaped(extended, F32)] + sends(3, 2, 3),
        scratch_shapes=[pltpu.VMEM(field, F32), inverse_scr] + [pltpu.VMEM(field, BF16)] * 4
        + [pltpu.VMEM((ROWS, COLS), jnp.int32), fold_scr, lon_scr, pltpu.VMEM((3, 2, ROWS, HALF), F32)]
        + staging(3) + [pltpu.SemaphoreType.DMA((6,)), quad_sems] + slot_sems,
        compiler_params=limit(62),
        cost_estimate=cost(work),
        name="vertical_first",
    )(lam, inverse, *coefs, depth)

    def ring(size, shift):
        return [(i, (i + shift) % size) for i in range(size)]

    def exchange(slots, north, south):
        near = lax.all_to_all(slots, "near", 0, 0, tiled=True)
        rims = [lax.ppermute(north, "lat", ring(lats, 1)), lax.ppermute(south, "lat", ring(lats, -1))]
        parts = slots.shape[1]
        north, south, *fars = pl.pallas_call(
            relay_kernel,
            in_specs=[smem] + [vmem] * 3,
            out_specs=[vmem] * 5,
            out_shape=[shaped(rim.shape, BF16) for rim in rims]
            + [shaped((size, ROWS, COLS), BF16) for size in (parts, QUADS, parts)],
            input_output_aliases={2: 0, 3: 1},
            compiler_params=limit(4),
            cost_estimate=cost(work),
            name="relay",
        )(fold_block, near, *rims)
        far = [lax.ppermute(part, lon, ring(count, NEAR * (step + 1))) for step, part in enumerate(fars)]
        return (north, south), (near, *far)

    def stencil(g, rims, rims_c):
        return pl.pallas_call(
            transposed_h,
            in_specs=[vmem] * 10,
            out_specs=vmem,
            out_shape=shaped(extended, F32),
            compiler_params=limit(4),
            cost_estimate=cost(work),
            name="horizontal",
        )(g, *coefs, depth, *rims, *rims_c)

    rims1, folds1 = exchange(*sent1)
    pre1 = stencil(g1, rims1, rims1)

    g2, *sent2, rim_c = pl.pallas_call(
        second_kernel,
        in_specs=[vmem, smem] + [vmem] * 4 + [hbm] + [vmem] * 3,
        out_specs=[vmem, hbm, vmem, vmem, vmem],
        out_shape=[shaped(extended, F32)] + sends(1, 1, 1) + [shaped((3, ROWS, COLS), F32)],
        scratch_shapes=[pltpu.VMEM(field, F32), inverse_scr, fold_scr, lon_scr] + staging(1) + [quad_sems] + slot_sems,
        compiler_params=limit(44),
        cost_estimate=cost(work),
        name="vertical_second",
    )(pre1, fold_block, *folds1, inverse, sn, mn, depth)

    rims2, folds2 = exchange(*sent2)
    pre2 = stencil(g2, rims2, rims1)

    return pl.pallas_call(
        last_kernel,
        in_specs=[vmem, smem] + [vmem] * 6,
        out_specs=hbm,
        out_shape=shaped(field, F32),
        scratch_shapes=[pltpu.VMEM(field, F32), pltpu.SemaphoreType.DMA((3,))],
        compiler_params=limit(4),
        name="add_fold",
    )(pre2, fold_block, *folds2, rim_c, depth)


def solution(mesh):
    lons, lats = mesh.devices.shape
    split = jax.sharding.Mesh(mesh.devices.reshape(lons // NEAR, NEAR, lats), ("far", "near", "lat"))
    lon = ("far", "near")
    field = P(None, "lat", lon)
    return jax.shard_map(
        per_device,
        mesh=split,
        in_specs=(field, P(None, None, "lat", lon), field, field, field, field, P("lat", lon), P()),
        out_specs=field,
        check_vma=False,
    )
```

```python
import jax
import jax.numpy as jnp
from jax import lax
from jax.experimental import pallas as pl
from jax.experimental.pallas import tpu as pltpu
from jax.sharding import PartitionSpec as P

F32 = jnp.float32
BF16 = jnp.bfloat16
LEV = 75
ROWS = 8
COLS = 256
HALF = 128
QUADS = 19
FULL_QUADS = 18
AHEAD = 4
TOGETHER = 6
NEAR = 8
OWN = LEV + 3
EXT = LEV + 6
TAIL = LEV - 4 * FULL_QUADS


def lane_ids():
    return lax.broadcasted_iota(jnp.int32, (ROWS, HALF), 1)


def row_ids():
    return lax.broadcasted_iota(jnp.int32, (ROWS, HALF), 0)


def turn(tile, shift, axis):
    size = tile.shape[axis]
    if isinstance(shift, int):
        shift = shift % size
        if shift == 0:
            return tile
    return pltpu.roll(tile, shift, axis)


def halves(value):
    return [value[:, :HALF], value[:, HALF:]]


def for_quads(body):
    def step(quad, carry):
        body(quad, 4)
        return carry

    lax.fori_loop(0, FULL_QUADS, step, 0)
    body(FULL_QUADS, TAIL)


def vertical_sums(inverse_ref, weighted_ref, first_level, count):
    sums = [None] * count
    for k in range(LEV):
        weight = weighted_ref[k]
        for jj in range(count):
            term = inverse_ref[k, first_level + jj].astype(F32) * weight
            sums[jj] = term if k == 0 else sums[jj] + term
    return sums


def sum_quads(inverse_ref, weighted_ref, depth, g_ref, levels_copy, pack):
    def sum_one(quad, count):
        sums = vertical_sums(inverse_ref, weighted_ref, quad * 4, count)
        for l in range(count):
            g_ref[quad * 4 + l] = jnp.where(depth > quad * 4 + l, sums[l], 0.0)

    def step(quad, carry):
        start_ahead(quad, levels_copy)
        levels_copy(quad, 4).wait()
        pack(jnp.maximum(quad - 1, 0), 4, lambda: sum_one(quad, 4))
        return carry

    lax.fori_loop(0, FULL_QUADS, step, 0)
    levels_copy(FULL_QUADS, TAIL).wait()
    pack(FULL_QUADS - 1, 4, lambda: sum_one(FULL_QUADS, TAIL))
    pack(FULL_QUADS, TAIL, None)


def place_lanes(acc_ref, side, quad, tiles, from_lane, ahead):
    which = quad // 16
    first = lax.rem(quad, 16) * 4
    lane = lane_ids()
    total = acc_ref[side, which]
    for l, tile in enumerate(tiles):
        spot = first + l
        rolled = pltpu.roll(tile, lax.rem(2 * spot + ahead + (2 * HALF - from_lane), HALF), 1)
        total = jnp.where((lane // 2) == lax.rem(spot + ahead // 2, 64), rolled, total)
    acc_ref[side, which] = total


def pack_quad(quad, count, g_ref, sn_ref, mn_ref, se_ref, me_ref, north_ref, south_ref,
              fold_scr, lon_scr, lonc_scr, with_coefs, beside=None):
    row = row_ids()
    gs = [g_ref[quad * 4 + l] for l in range(count)]
    is_top = lax.axis_index("lat") == lax.axis_size("lat") - 1

    def gathered(tiles_of, shift, ahead=0):
        for c in range(2):
            value = jnp.zeros((ROWS, HALF), F32)
            for l in range(count):
                moved = turn(tiles_of(l)[c], 2 * l + 2 * ahead - shift, 0)
                value = jnp.where((row // 2) == (l + ahead) % 4, moved, value)
            yield slice(c * HALF, (c + 1) * HALF), value

    def level_of(ref):
        return lambda l: halves(ref[quad * 4 + l].astype(F32))

    def far_of(l, c):
        g = halves(gs[l])[c]
        return level_of(sn_ref)(l)[c] * ((turn(g, -1, 0) - g) * (1.0 / 12.0))

    def south_rows(l):
        return [jnp.where(row == 0, halves(gs[l])[c], turn(far_of(l, c), 1, 0)) for c in range(2)]

    def north_rows(l):
        return [jnp.where(row == 7, halves(gs[l])[c], far_of(l, c)) for c in range(2)]

    def north_coefs(l):
        return [jnp.where(row == 7, level_of(sn_ref)(l)[c], turn(level_of(mn_ref)(l)[c], -1, 0)) for c in range(2)]

    for cols, value in gathered(south_rows, 0, 1):
        south_ref[0, quad, :, cols] = value.astype(BF16)
    place_lanes(lon_scr, 0, quad, [g[:, HALF:] for g in gs], 126, 0)
    place_lanes(lon_scr, 1, quad, [g[:, :HALF] for g in gs], 0, 2)
    if with_coefs:
        se = [level_of(se_ref)(l) for l in range(count)]
        me = [level_of(me_ref)(l)[1] for l in range(count)]
        place_lanes(lonc_scr, 0, quad, [tile[1] for tile in se], 126, 0)
        place_lanes(lonc_scr, 2, quad, me, 126, 0)
        place_lanes(lonc_scr, 1, quad, [tile[0] for tile in se], 0, 2)
    if beside is not None:
        beside()

    @pl.when(jnp.logical_not(is_top))
    def _():
        for cols, value in gathered(north_rows, 6):
            north_ref[0, quad, :, cols] = value.astype(BF16)
        if with_coefs:
            for cols, value in gathered(north_coefs, 6):
                north_ref[1, quad, :, cols] = value.astype(BF16)

    @pl.when(is_top)
    def _():
        def ghosts(l):
            g = halves(gs[l])
            s = level_of(sn_ref)(l)
            m = level_of(mn_ref)(l)
            result = []
            for c in range(2):
                slope = s[c] * (1.0 / 12.0)
                direct = g[c] * (m[c] - 7.0 * slope)
                inner = (g[c] - turn(g[c], -1, 0)) * slope
                result.append(jnp.where(row == 7, direct + turn(inner, 1, 0), turn(slope * g[c], -1, 0)))
            return result

        for cols, value in gathered(ghosts, 6):
            fold_scr[quad, :, cols] = value


def fill_sends(slots_hbm, fold_scr, lon_scr, lonc_scr, flipped_scr, rim_scr, slot_sem, rim_sem):
    near = lax.axis_index("near")
    is_top = lax.axis_index("lat") == lax.axis_size("lat") - 1
    parts = rim_scr.shape[1]
    folds = [pltpu.make_async_copy(flipped_scr, slots_hbm.at[i, pl.ds(0, QUADS)], slot_sem.at[i])
             for i in range(NEAR)]
    rims = [pltpu.make_async_copy(rim_scr.at[side], slots_hbm.at[slot, pl.ds(QUADS, parts)], rim_sem.at[side])
            for side, slot in enumerate((lax.rem(near + 1, NEAR), lax.rem(near + NEAR - 1, NEAR)))]
    for side in range(2):
        for part, (ref, which) in enumerate(((lon_scr, side), (lonc_scr, side), (lonc_scr, 2))[:parts]):
            rim_scr[side, part] = jnp.concatenate([ref[which, 0], ref[which, 1]], axis=1).astype(BF16)
        rims[side].start()

    @pl.when(is_top)
    def _():
        r = lax.broadcasted_iota(jnp.int32, (COLS, COLS), 0)
        q = lax.broadcasted_iota(jnp.int32, (COLS, COLS), 1)
        mirror = (r + q == COLS - 1).astype(F32).astype(BF16)
        flat = fold_scr[...].reshape(20 * ROWS, COLS).astype(BF16)
        flipped = jnp.dot(flat, mirror, preferred_element_type=F32).reshape(20, ROWS, COLS)
        flipped_scr[...] = flipped[:QUADS].astype(BF16)
        for copy in folds:
            copy.start()
        for copy in folds:
            copy.wait()

    for copy in rims:
        copy.wait()


def transposed_h(g_ref, se_ref, me_ref, sn_ref, mn_ref, depth_ref, north_ref, south_ref,
                 north_c_ref, out_ref):
    row = row_ids()
    lane = lane_ids()
    lat = lax.axis_index("lat")
    has_south = lat > 0
    has_north = lat < lax.axis_size("lat") - 1

    def kept(value, condition):
        return halves(jnp.where(condition, value.astype(F32), 0.0))

    def quad_body(quad, levels):
        g_n = kept(north_ref[0, quad], has_south)
        c_n = kept(north_c_ref[1, quad], has_south)
        g_s = kept(south_ref[0, quad], has_north)
        ready = []
        for l in range(levels):
            j = quad * 4 + l
            depth = halves(depth_ref[...])
            g = halves(g_ref[j])
            se = halves(se_ref[j].astype(F32))
            me = halves(me_ref[j].astype(F32))
            sn = halves(sn_ref[j].astype(F32))
            mn = halves(mn_ref[j].astype(F32))
            nothing = jnp.zeros((ROWS, HALF), F32)
            tiles = [g[0], g[1], nothing]
            jump = [turn(jnp.where(lane == 0, tiles[c + 1], tiles[c]), -1, 1) - tiles[c] for c in range(2)]
            speeds = [se[0], se[1]]
            mixes = [me[0], me[1]]
            far = [speeds[c] * (jump[c] * (1.0 / 12.0)) for c in range(2)] + [nothing]
            seven = [7.0 * far[c] for c in range(2)]
            mixed = [mixes[c] * jump[c] for c in range(2)]
            high = [seven[c] - mixed[c] for c in range(2)] + [nothing]
            total = []
            for c in range(2):
                before = (c + 2) % 3
                after = c + 1
                value = g[c] + seven[c] + mixed[c]
                value = value + turn(jnp.where(lane == 127, high[before], high[c]), 1, 1)
                value = value - turn(jnp.where(lane == 0, far[after], far[c]), -1, 1)
                value = value - turn(jnp.where(lane >= 126, far[before], far[c]), 2, 1)
                total.append(value)
            for c in range(2):
                pair = (row // 2) == l
                rim = turn(jnp.where(pair, g_n[c], g_s[c]), 6 - 2 * l, 0)
                s_r = turn(c_n[c], 6 - 2 * l, 0)
                m_r = turn(s_r, 1, 0)
                d = turn(jnp.where(row == 0, rim, g[c]), -1, 0) - g[c]
                d_r = turn(jnp.where(row == 0, g[c], rim), -1, 0) - rim
                fa = sn[c] * (d * (1.0 / 12.0))
                fa_r = jnp.where(row == 7, s_r * (d_r * (1.0 / 12.0)), jnp.where(row == 6, rim, turn(rim, -1, 0)))
                seven_y = 7.0 * fa
                mixed_y = mn[c] * d
                hi = seven_y - mixed_y
                hi_r = 7.0 * fa_r - m_r * d_r
                value = total[c] + seven_y + mixed_y
                value = value + turn(jnp.where(row == 7, hi_r, hi), 1, 0)
                value = value - turn(jnp.where(row == 0, fa_r, fa), -1, 0)
                value = value - turn(jnp.where(row >= 6, fa_r, fa), 2, 0)
                ready.append((j, c, jnp.where(depth[c] > j, value, 0.0)))
        for j, c, value in ready:
            out_ref[j, :, c * HALF:(c + 1) * HALF] = value

    for_quads(quad_body)
    for part in range(LEV, EXT):
        out_ref[part] = g_ref[part]


def lon_rims(near_ref, far1_ref, far3_ref, part):
    near = lax.axis_index("near")
    west = near_ref[lax.rem(near + NEAR - 1, NEAR), QUADS + part].astype(F32)
    east = near_ref[lax.rem(near + 1, NEAR), QUADS + part].astype(F32)
    west = jnp.where(near == 0, far1_ref[QUADS + part].astype(F32), west)
    east = jnp.where(near == NEAR - 1, far3_ref[QUADS + part].astype(F32), east)
    return west, east


def lon_edges(west_g, east_g, west_s, west_m, east_s, own_ref):
    lane = lane_ids()
    west_edge, east_edge = [], []
    even = lane % 2 == 0

    for w, e, own, w_s, w_m, e_s, o_s, o_m in zip(*map(halves, (
            west_g, east_g, own_ref[LEV], west_s, west_m, east_s, own_ref[LEV + 1], own_ref[LEV + 2]))):
        jump_w = jnp.where(even, turn(w, -1, 1), turn(own, -1, 1)) - w
        far_w = w_s * (jump_w * (1.0 / 12.0))
        high_w = 7.0 * far_w - w_m * jump_w
        west_edge.append(turn(jnp.where(even, turn(high_w, -1, 1) - far_w, -far_w), 2, 1))
        next_e = turn(e, -1, 1)
        far_e = e_s * ((next_e - e) * (1.0 / 12.0))
        far_o = o_s * (next_e * (1.0 / 12.0))
        east_edge.append(jnp.where(even, -turn(far_o, -1, 1), 7.0 * far_o + o_m * next_e - turn(far_e, -1, 1)))
    return west_edge, east_edge


def place_of(block):
    return block // NEAR, lax.rem(block, NEAR)


def add_fold(pre_ref, fold_ref, near_ref, far_refs, rim_c, depth_ref, put, after=None):
    row = row_ids()
    lane = lane_ids()
    west_g, east_g = lon_rims(near_ref, far_refs[0], far_refs[2], 0)
    west_edge, east_edge = lon_edges(west_g, east_g, *rim_c, pre_ref)
    depth = halves(depth_ref[...])
    on_top = lax.axis_index("lat") == lax.axis_size("lat") - 1
    fars = lax.axis_size("far")
    my_far = lax.axis_index("far")
    far, near = place_of(fold_ref[my_far * NEAR + lax.axis_index("near")])
    steps = lax.rem(my_far - far + fars, fars)

    def quad_values(quad, levels):
        fold = near_ref[near, quad].astype(F32)
        for step, ref in enumerate(far_refs):
            fold = jnp.where(steps == step + 1, ref[quad].astype(F32), fold)
        fold = halves(fold)
        ready = []
        for l in range(levels):
            j = quad * 4 + l
            first = j < 64
            spot = lax.rem(j, 64)
            edge = jnp.where((lane // 2) == spot, jnp.where(first, east_edge[0], east_edge[1]),
                             jnp.where(first, west_edge[0], west_edge[1]))
            edge = pltpu.roll(edge, lax.rem(2 * HALF - 2 - 2 * spot, HALF), 1)
            for c in range(2):
                cols = slice(c * HALF, (c + 1) * HALF)
                at_edge = lane < 2 if c == 0 else lane >= 126
                more = jnp.where(at_edge, edge, 0.0)
                more = more + jnp.where(((row == 5) | (row == 6)) & on_top, turn(fold[c], 5 - 2 * l, 0), 0.0)
                ready.append((j, cols, pre_ref[j, :, cols] + jnp.where(depth[c] > j, more, 0.0)))
        return ready

    def several(step, carry):
        ready = []
        for part in range(TOGETHER):
            ready += quad_values(step * TOGETHER + part, 4)
        for j, cols, value in ready:
            put(j, cols, value)
        if after is not None:
            after(step * TOGETHER + TOGETHER - 1)
        return carry

    lax.fori_loop(0, FULL_QUADS // TOGETHER, several, 0)
    for j, cols, value in quad_values(FULL_QUADS, TAIL):
        put(j, cols, value)
    if after is not None:
        after(FULL_QUADS)


def start_ahead(quad, levels_copy):
    @pl.when(quad + AHEAD < FULL_QUADS)
    def _():
        levels_copy(quad + AHEAD, 4).start()

    @pl.when(quad + AHEAD == FULL_QUADS)
    def _():
        levels_copy(FULL_QUADS, TAIL).start()


def first_kernel(lam_hbm, inv_hbm, se_hbm, me_hbm, sn_hbm, mn_hbm, depth_hbm,
                 g_ref, slots_hbm, north_ref, south_ref,
                 lam, inverse, se, me, sn, mn, depth_ref, fold_scr, lon_scr, lonc_scr,
                 flipped_scr, rim_scr, small_sem, sem, slot_sem, rim_sem):
    small = [pltpu.make_async_copy(src, dst, small_sem.at[i])
             for i, (src, dst) in enumerate([(depth_hbm, depth_ref), (lam_hbm, lam), (sn_hbm, sn),
                                             (mn_hbm, mn), (se_hbm, se), (me_hbm, me)])]

    def levels_copy(quad, count):
        part = pl.ds(quad * 4, count)
        return pltpu.make_async_copy(inv_hbm.at[:, part], inverse.at[:, part], sem.at[quad])

    small[0].start()
    small[1].start()
    levels_copy(0, 4).start()
    levels_copy(1, 4).start()
    for copy in small[2:]:
        copy.start()
    for quad in range(2, AHEAD):
        levels_copy(quad, 4).start()
    small[0].wait()
    small[1].wait()
    depth = depth_ref[...]

    def mask(k, carry):
        lam[k] = jnp.where(depth > k, lam[k], 0.0)
        return carry

    lax.fori_loop(0, LEV, mask, 0, unroll=5)
    for copy in small[2:]:
        copy.wait()

    def pack(quad, count, beside):
        pack_quad(quad, count, g_ref, sn, mn, se, me, north_ref, south_ref, fold_scr, lon_scr, lonc_scr, True, beside)

    sum_quads(inverse, lam, depth, g_ref, levels_copy, pack)
    for part, (ref, side) in enumerate(((lon_scr, 1), (lonc_scr, 0), (lonc_scr, 2))):
        g_ref[LEV + part] = jnp.concatenate([ref[side, 0], ref[side, 1]], axis=1)
    fill_sends(slots_hbm, fold_scr, lon_scr, lonc_scr, flipped_scr, rim_scr, slot_sem, rim_sem)


def second_kernel(pre_ref, fold_ref, near_ref, far1_ref, far2_ref, far3_ref,
                  inv_hbm, sn_ref, mn_ref, depth_ref,
                  g_ref, slots_hbm, north_ref, south_ref,
                  lam, inverse, fold_scr, lon_scr, flipped_scr, rim_scr, sem, slot_sem, rim_sem):
    def levels_copy(quad, count):
        part = pl.ds(quad * 4, count)
        return pltpu.make_async_copy(inv_hbm.at[:, part], inverse.at[:, part], sem.at[quad])

    for quad in range(AHEAD):
        levels_copy(quad, 4).start()

    def put(j, cols, value):
        lam[j, :, cols] = value

    west_s, east_s = lon_rims(near_ref, far1_ref, far3_ref, 1)
    west_m, _ = lon_rims(near_ref, far1_ref, far3_ref, 2)
    for part, tile in enumerate((west_s, west_m, east_s)):
        g_ref[OWN + part] = tile
    add_fold(pre_ref, fold_ref, near_ref, (far1_ref, far2_ref, far3_ref), (west_s, west_m, east_s), depth_ref, put)
    depth = depth_ref[...]

    def pack(quad, count, beside):
        pack_quad(quad, count, g_ref, sn_ref, mn_ref, None, None, north_ref, south_ref, fold_scr, lon_scr, None, False,
                  beside)

    sum_quads(inverse, lam, depth, g_ref, levels_copy, pack)
    g_ref[LEV] = jnp.concatenate([lon_scr[1, 0], lon_scr[1, 1]], axis=1)
    for part in range(LEV + 1, OWN):
        g_ref[part] = pre_ref[part]
    fill_sends(slots_hbm, fold_scr, lon_scr, None, flipped_scr, rim_scr, slot_sem, rim_sem)


def last_kernel(pre_ref, fold_ref, near_ref, far1_ref, far2_ref, far3_ref,
                depth_ref, out_hbm, total, sem):
    copies = [pltpu.make_async_copy(total.at[pl.ds(start, size)], out_hbm.at[pl.ds(start, size)], sem.at[i])
              for i, (start, size) in enumerate(((0, 24), (24, 24), (48, 27)))]

    def put(j, cols, value):
        total[j, :, cols] = value

    def after(quad):
        for i, last in enumerate((5, 11, FULL_QUADS)):
            @pl.when(quad == last)
            def _(copy=copies[i]):
                copy.start()

    add_fold(pre_ref, fold_ref, near_ref, (far1_ref, far2_ref, far3_ref),
             [pre_ref[part] for part in range(OWN, EXT)], depth_ref, put, after)
    for copy in copies:
        copy.wait()


def relay_kernel(fold_ref, near_ref, *refs):
    fars = lax.axis_size("far")
    my_far = lax.axis_index("far")
    my_near = lax.axis_index("near")
    far1_ref, _, far3_ref = refs[-3:]
    for ref, slot in ((far1_ref, lax.rem(my_near + NEAR - 1, NEAR)), (far3_ref, lax.rem(my_near + 1, NEAR))):
        for part in range(QUADS, ref.shape[0]):
            ref[part] = near_ref[slot, part]

    @pl.when(lax.axis_index("lat") == lax.axis_size("lat") - 1)
    def _():
        for step, out_ref in enumerate(refs[-3:]):
            target = lax.rem(my_far + step + 1, fars)
            _, near = place_of(fold_ref[target * NEAR + my_near])
            for quad in range(QUADS):
                out_ref[quad] = near_ref[near, quad]


def shaped(shape, dtype):
    return jax.ShapeDtypeStruct(shape, dtype)


def per_device(lam, inverse, se, me, sn, mn, depth, fold_block):
    field = (LEV, ROWS, COLS)
    extended = (EXT, ROWS, COLS)
    lats = lax.axis_size("lat")
    count = lax.axis_size("far") * NEAR
    lon = ("far", "near")
    vmem = pl.BlockSpec(memory_space=pltpu.VMEM)
    hbm = pl.BlockSpec(memory_space=pltpu.HBM)
    smem = pl.BlockSpec(memory_space=pltpu.SMEM)
    coefs = [se, me, sn, mn]
    lon_scr = pltpu.VMEM((2, 2, ROWS, HALF), F32)
    fold_scr = pltpu.VMEM((20, ROWS, COLS), F32)
    inverse_scr = pltpu.VMEM((LEV,) + field, BF16)
    quad_sems = pltpu.SemaphoreType.DMA((QUADS,))
    slot_sems = [pltpu.SemaphoreType.DMA((NEAR,)), pltpu.SemaphoreType.DMA((2,))]
    work = 2 * LEV * LEV * ROWS * COLS
    mib = 1024 * 1024
    block = (QUADS, ROWS, COLS)

    def cost(bytes_accessed):
        return pl.CostEstimate(flops=work, bytes_accessed=bytes_accessed, transcendentals=0)

    def limit(size):
        return pltpu.CompilerParams(vmem_limit_bytes=size * mib)

    def sends(north, south, parts):
        return [shaped((NEAR, QUADS + parts, ROWS, COLS), BF16), shaped((north,) + block, BF16),
                shaped((south,) + block, BF16)]

    def staging(parts):
        return [pltpu.VMEM(block, BF16), pltpu.VMEM((2, parts, ROWS, COLS), BF16)]

    g1, *sent1 = pl.pallas_call(
        first_kernel,
        in_specs=[hbm] * 7,
        out_specs=[vmem, hbm, vmem, vmem],
        out_shape=[shaped(extended, F32)] + sends(2, 1, 3),
        scratch_shapes=[pltpu.VMEM(field, F32), inverse_scr] + [pltpu.VMEM(field, BF16)] * 4
        + [pltpu.VMEM((ROWS, COLS), jnp.int32), fold_scr, lon_scr, pltpu.VMEM((3, 2, ROWS, HALF), F32)]
        + staging(3) + [pltpu.SemaphoreType.DMA((6,)), quad_sems] + slot_sems,
        compiler_params=limit(62),
        cost_estimate=cost(work),
        name="vertical_first",
    )(lam, inverse, *coefs, depth)

    def ring(size, shift):
        return [(i, (i + shift) % size) for i in range(size)]

    def exchange(g, slots, north, south, *carried):
        near = lax.all_to_all(slots, "near", 0, 0, tiled=True)
        rims = [lax.ppermute(north, "lat", ring(lats, 1)), lax.ppermute(south, "lat", ring(lats, -1))]
        parts = slots.shape[1]
        held = len(carried)
        g, north, south, *rest = pl.pallas_call(
            relay_kernel,
            in_specs=[smem] + [vmem] * (4 + held),
            out_specs=[vmem] * (6 + held),
            out_shape=[shaped(extended, F32)] + [shaped(part.shape, BF16) for part in (*rims, *carried)]
            + [shaped((size, ROWS, COLS), BF16) for size in (parts, QUADS, parts)],
            input_output_aliases={2 + i: i for i in range(3 + held)},
            compiler_params=limit(4),
            cost_estimate=cost(work),
            name="relay",
        )(fold_block, near, g, *rims, *carried)
        carried, fars = rest[:held], rest[held:]
        far = [lax.ppermute(part, lon, ring(count, NEAR * (step + 1))) for step, part in enumerate(fars)]
        return g, (north, south), (near, *far), carried

    def stencil(g, rims, north_c):
        return pl.pallas_call(
            transposed_h,
            in_specs=[vmem] * 9,
            out_specs=vmem,
            out_shape=shaped(extended, F32),
            compiler_params=limit(4),
            cost_estimate=cost(work),
            name="horizontal",
        )(g, *coefs, depth, *rims, north_c)

    g1, rims1, folds1, _ = exchange(g1, *sent1)
    pre1 = stencil(g1, rims1, rims1[0])

    g2, *sent2 = pl.pallas_call(
        second_kernel,
        in_specs=[vmem, smem] + [vmem] * 4 + [hbm] + [vmem] * 3,
        out_specs=[vmem, hbm, vmem, vmem],
        out_shape=[shaped(extended, F32)] + sends(1, 1, 1),
        scratch_shapes=[pltpu.VMEM(field, F32), inverse_scr, fold_scr, lon_scr] + staging(1) + [quad_sems] + slot_sems,
        compiler_params=limit(36),
        cost_estimate=cost(work),
        name="vertical_second",
    )(pre1, fold_block, *folds1, inverse, sn, mn, depth)

    g2, rims2, folds2, (north_c,) = exchange(g2, *sent2, rims1[0])
    pre2 = stencil(g2, rims2, north_c)

    return pl.pallas_call(
        last_kernel,
        in_specs=[vmem, smem] + [vmem] * 5,
        out_specs=hbm,
        out_shape=shaped(field, F32),
        scratch_shapes=[pltpu.VMEM(field, F32), pltpu.SemaphoreType.DMA((3,))],
        compiler_params=limit(4),
        name="add_fold",
    )(pre2, fold_block, *folds2, depth)


def solution(mesh):
    lons, lats = mesh.devices.shape
    split = jax.sharding.Mesh(mesh.devices.reshape(lons // NEAR, NEAR, lats), ("far", "near", "lat"))
    lon = ("far", "near")
    field = P(None, "lat", lon)
    return jax.shard_map(
        per_device,
        mesh=split,
        in_specs=(field, P(None, None, "lat", lon), field, field, field, field, P("lat", lon), P()),
        out_specs=field,
        check_vma=False,
    )
```

```python
import jax
import jax.numpy as jnp
from jax import lax
from jax.experimental import pallas as pl
from jax.experimental.pallas import tpu as pltpu
from jax.sharding import PartitionSpec as P

F32 = jnp.float32
BF16 = jnp.bfloat16
LEV = 75
ROWS = 8
COLS = 256
HALF = 128
QUADS = 19
FULL_QUADS = 18
AHEAD = 5
TOGETHER = 6
NEAR = 8
OWN = LEV + 3
EXT = LEV + 6
TAIL = LEV - 4 * FULL_QUADS


def lane_ids():
    return lax.broadcasted_iota(jnp.int32, (ROWS, HALF), 1)


def row_ids():
    return lax.broadcasted_iota(jnp.int32, (ROWS, HALF), 0)


def turn(tile, shift, axis):
    size = tile.shape[axis]
    if isinstance(shift, int):
        shift = shift % size
        if shift == 0:
            return tile
    return pltpu.roll(tile, shift, axis)


def halves(value):
    return [value[:, :HALF], value[:, HALF:]]


def for_quads(body):
    def step(quad, carry):
        body(quad, 4)
        return carry

    lax.fori_loop(0, FULL_QUADS, step, 0)
    body(FULL_QUADS, TAIL)


def vertical_sums(inverse_ref, weighted_ref, first_level, count):
    sums = [None] * count
    for k in range(LEV):
        weight = weighted_ref[k]
        for jj in range(count):
            term = inverse_ref[k, first_level + jj].astype(F32) * weight
            sums[jj] = term if k == 0 else sums[jj] + term
    return sums


def sum_quads(inverse_ref, weighted_ref, depth, g_ref, levels_copy, pack):
    def sum_one(quad, count):
        sums = vertical_sums(inverse_ref, weighted_ref, quad * 4, count)
        for l in range(count):
            g_ref[quad * 4 + l] = jnp.where(depth > quad * 4 + l, sums[l], 0.0)

    def step(quad, carry):
        start_ahead(quad, levels_copy)
        levels_copy(quad, 4).wait()
        pack(jnp.maximum(quad - 1, 0), 4, lambda: sum_one(quad, 4))
        return carry

    lax.fori_loop(0, FULL_QUADS, step, 0)
    levels_copy(FULL_QUADS, TAIL).wait()
    pack(FULL_QUADS - 1, 4, lambda: sum_one(FULL_QUADS, TAIL))
    pack(FULL_QUADS, TAIL, None)


def place_lanes(acc_ref, side, quad, tiles, from_lane, ahead):
    which = quad // 16
    first = lax.rem(quad, 16) * 4
    lane = lane_ids()
    total = acc_ref[side, which]
    for l, tile in enumerate(tiles):
        spot = first + l
        rolled = pltpu.roll(tile, lax.rem(2 * spot + ahead + (2 * HALF - from_lane), HALF), 1)
        total = jnp.where((lane // 2) == lax.rem(spot + ahead // 2, 64), rolled, total)
    acc_ref[side, which] = total


def pack_quad(quad, count, g_ref, sn_ref, mn_ref, se_ref, me_ref, north_ref, south_ref,
              fold_scr, lon_scr, lonc_scr, with_coefs, beside=None):
    row = row_ids()
    gs = [g_ref[quad * 4 + l] for l in range(count)]
    is_top = lax.axis_index("lat") == lax.axis_size("lat") - 1

    def gathered(tiles_of, shift, ahead=0):
        for c in range(2):
            value = jnp.zeros((ROWS, HALF), F32)
            for l in range(count):
                moved = turn(tiles_of(l)[c], 2 * l + 2 * ahead - shift, 0)
                value = jnp.where((row // 2) == (l + ahead) % 4, moved, value)
            yield slice(c * HALF, (c + 1) * HALF), value

    def level_of(ref):
        return lambda l: halves(ref[quad * 4 + l].astype(F32))

    def far_of(l, c):
        g = halves(gs[l])[c]
        return level_of(sn_ref)(l)[c] * ((turn(g, -1, 0) - g) * (1.0 / 12.0))

    def south_rows(l):
        return [jnp.where(row == 0, halves(gs[l])[c], turn(far_of(l, c), 1, 0)) for c in range(2)]

    def north_rows(l):
        return [jnp.where(row == 7, halves(gs[l])[c], far_of(l, c)) for c in range(2)]

    def north_coefs(l):
        return [jnp.where(row == 7, level_of(sn_ref)(l)[c], turn(level_of(mn_ref)(l)[c], -1, 0)) for c in range(2)]

    for cols, value in gathered(south_rows, 0, 1):
        south_ref[0, quad, :, cols] = value.astype(BF16)
    place_lanes(lon_scr, 0, quad, [g[:, HALF:] for g in gs], 126, 0)
    place_lanes(lon_scr, 1, quad, [g[:, :HALF] for g in gs], 0, 2)
    if with_coefs:
        se = [level_of(se_ref)(l) for l in range(count)]
        me = [level_of(me_ref)(l)[1] for l in range(count)]
        place_lanes(lonc_scr, 0, quad, [tile[1] for tile in se], 126, 0)
        place_lanes(lonc_scr, 2, quad, me, 126, 0)
        place_lanes(lonc_scr, 1, quad, [tile[0] for tile in se], 0, 2)
    if beside is not None:
        beside()

    @pl.when(jnp.logical_not(is_top))
    def _():
        for cols, value in gathered(north_rows, 6):
            north_ref[0, quad, :, cols] = value.astype(BF16)
        if with_coefs:
            for cols, value in gathered(north_coefs, 6):
                north_ref[1, quad, :, cols] = value.astype(BF16)

    @pl.when(is_top)
    def _():
        def ghosts(l):
            g = halves(gs[l])
            s = level_of(sn_ref)(l)
            m = level_of(mn_ref)(l)
            result = []
            for c in range(2):
                slope = s[c] * (1.0 / 12.0)
                direct = g[c] * (m[c] - 7.0 * slope)
                inner = (g[c] - turn(g[c], -1, 0)) * slope
                result.append(jnp.where(row == 7, direct + turn(inner, 1, 0), turn(slope * g[c], -1, 0)))
            return result

        for cols, value in gathered(ghosts, 6):
            fold_scr[quad, :, cols] = value


def fill_sends(slots_hbm, fold_scr, lon_scr, lonc_scr, flipped_scr, rim_scr, slot_sem, rim_sem):
    near = lax.axis_index("near")
    is_top = lax.axis_index("lat") == lax.axis_size("lat") - 1
    parts = rim_scr.shape[1]
    folds = [pltpu.make_async_copy(flipped_scr, slots_hbm.at[i, pl.ds(0, QUADS)], slot_sem.at[i])
             for i in range(NEAR)]
    rims = [pltpu.make_async_copy(rim_scr.at[side], slots_hbm.at[slot, pl.ds(QUADS, parts)], rim_sem.at[side])
            for side, slot in enumerate((lax.rem(near + 1, NEAR), lax.rem(near + NEAR - 1, NEAR)))]
    for side in range(2):
        for part, (ref, which) in enumerate(((lon_scr, side), (lonc_scr, side), (lonc_scr, 2))[:parts]):
            rim_scr[side, part] = jnp.concatenate([ref[which, 0], ref[which, 1]], axis=1).astype(BF16)
        rims[side].start()

    @pl.when(is_top)
    def _():
        r = lax.broadcasted_iota(jnp.int32, (COLS, COLS), 0)
        q = lax.broadcasted_iota(jnp.int32, (COLS, COLS), 1)
        mirror = (r + q == COLS - 1).astype(F32).astype(BF16)
        flat = fold_scr[...].reshape(20 * ROWS, COLS).astype(BF16)
        flipped = jnp.dot(flat, mirror, preferred_element_type=F32).reshape(20, ROWS, COLS)
        flipped_scr[...] = flipped[:QUADS].astype(BF16)
        for copy in folds:
            copy.start()
        for copy in folds:
            copy.wait()

    for copy in rims:
        copy.wait()


def transposed_h(g_ref, se_ref, me_ref, sn_ref, mn_ref, depth_ref, north_ref, south_ref,
                 north_c_ref, out_ref):
    row = row_ids()
    lane = lane_ids()
    lat = lax.axis_index("lat")
    has_south = lat > 0
    has_north = lat < lax.axis_size("lat") - 1

    def kept(value, condition):
        return halves(jnp.where(condition, value.astype(F32), 0.0))

    def quad_body(quad, levels):
        g_n = kept(north_ref[0, quad], has_south)
        c_n = kept(north_c_ref[1, quad], has_south)
        g_s = kept(south_ref[0, quad], has_north)
        ready = []
        for l in range(levels):
            j = quad * 4 + l
            depth = halves(depth_ref[...])
            g = halves(g_ref[j])
            se = halves(se_ref[j].astype(F32))
            me = halves(me_ref[j].astype(F32))
            sn = halves(sn_ref[j].astype(F32))
            mn = halves(mn_ref[j].astype(F32))
            nothing = jnp.zeros((ROWS, HALF), F32)
            tiles = [g[0], g[1], nothing]
            jump = [turn(jnp.where(lane == 0, tiles[c + 1], tiles[c]), -1, 1) - tiles[c] for c in range(2)]
            speeds = [se[0], se[1]]
            mixes = [me[0], me[1]]
            far = [speeds[c] * (jump[c] * (1.0 / 12.0)) for c in range(2)] + [nothing]
            seven = [7.0 * far[c] for c in range(2)]
            mixed = [mixes[c] * jump[c] for c in range(2)]
            high = [seven[c] - mixed[c] for c in range(2)] + [nothing]
            total = []
            for c in range(2):
                before = (c + 2) % 3
                after = c + 1
                value = g[c] + seven[c] + mixed[c]
                value = value + turn(jnp.where(lane == 127, high[before], high[c]), 1, 1)
                value = value - turn(jnp.where(lane == 0, far[after], far[c]), -1, 1)
                value = value - turn(jnp.where(lane >= 126, far[before], far[c]), 2, 1)
                total.append(value)
            for c in range(2):
                pair = (row // 2) == l
                rim = turn(jnp.where(pair, g_n[c], g_s[c]), 6 - 2 * l, 0)
                s_r = turn(c_n[c], 6 - 2 * l, 0)
                m_r = turn(s_r, 1, 0)
                d = turn(jnp.where(row == 0, rim, g[c]), -1, 0) - g[c]
                d_r = turn(jnp.where(row == 0, g[c], rim), -1, 0) - rim
                fa = sn[c] * (d * (1.0 / 12.0))
                fa_r = jnp.where(row == 7, s_r * (d_r * (1.0 / 12.0)), jnp.where(row == 6, rim, turn(rim, -1, 0)))
                seven_y = 7.0 * fa
                mixed_y = mn[c] * d
                hi = seven_y - mixed_y
                hi_r = 7.0 * fa_r - m_r * d_r
                value = total[c] + seven_y + mixed_y
                value = value + turn(jnp.where(row == 7, hi_r, hi), 1, 0)
                value = value - turn(jnp.where(row == 0, fa_r, fa), -1, 0)
                value = value - turn(jnp.where(row >= 6, fa_r, fa), 2, 0)
                ready.append((j, c, jnp.where(depth[c] > j, value, 0.0)))
        for j, c, value in ready:
            out_ref[j, :, c * HALF:(c + 1) * HALF] = value

    for_quads(quad_body)
    for part in range(LEV, EXT):
        out_ref[part] = g_ref[part]


def lon_rims(near_ref, far1_ref, far3_ref, part):
    near = lax.axis_index("near")
    west = near_ref[lax.rem(near + NEAR - 1, NEAR), QUADS + part].astype(F32)
    east = near_ref[lax.rem(near + 1, NEAR), QUADS + part].astype(F32)
    west = jnp.where(near == 0, far1_ref[QUADS + part].astype(F32), west)
    east = jnp.where(near == NEAR - 1, far3_ref[QUADS + part].astype(F32), east)
    return west, east


def lon_edges(west_g, east_g, west_s, west_m, east_s, own_ref):
    lane = lane_ids()
    west_edge, east_edge = [], []
    even = lane % 2 == 0

    for w, e, own, w_s, w_m, e_s, o_s, o_m in zip(*map(halves, (
            west_g, east_g, own_ref[LEV], west_s, west_m, east_s, own_ref[LEV + 1], own_ref[LEV + 2]))):
        jump_w = jnp.where(even, turn(w, -1, 1), turn(own, -1, 1)) - w
        far_w = w_s * (jump_w * (1.0 / 12.0))
        high_w = 7.0 * far_w - w_m * jump_w
        west_edge.append(turn(jnp.where(even, turn(high_w, -1, 1) - far_w, -far_w), 2, 1))
        next_e = turn(e, -1, 1)
        far_e = e_s * ((next_e - e) * (1.0 / 12.0))
        far_o = o_s * (next_e * (1.0 / 12.0))
        east_edge.append(jnp.where(even, -turn(far_o, -1, 1), 7.0 * far_o + o_m * next_e - turn(far_e, -1, 1)))
    return west_edge, east_edge


def place_of(block):
    return block // NEAR, lax.rem(block, NEAR)


def add_fold(pre_ref, fold_ref, near_ref, far_refs, rim_c, depth_ref, put, after=None):
    row = row_ids()
    lane = lane_ids()
    west_g, east_g = lon_rims(near_ref, far_refs[0], far_refs[2], 0)
    west_edge, east_edge = lon_edges(west_g, east_g, *rim_c, pre_ref)
    depth = halves(depth_ref[...])
    on_top = lax.axis_index("lat") == lax.axis_size("lat") - 1
    fars = lax.axis_size("far")
    my_far = lax.axis_index("far")
    far, near = place_of(fold_ref[my_far * NEAR + lax.axis_index("near")])
    steps = lax.rem(my_far - far + fars, fars)

    def quad_values(quad, levels):
        fold = near_ref[near, quad].astype(F32)
        for step, ref in enumerate(far_refs):
            fold = jnp.where(steps == step + 1, ref[quad].astype(F32), fold)
        fold = halves(fold)
        ready = []
        for l in range(levels):
            j = quad * 4 + l
            first = j < 64
            spot = lax.rem(j, 64)
            edge = jnp.where((lane // 2) == spot, jnp.where(first, east_edge[0], east_edge[1]),
                             jnp.where(first, west_edge[0], west_edge[1]))
            edge = pltpu.roll(edge, lax.rem(2 * HALF - 2 - 2 * spot, HALF), 1)
            for c in range(2):
                cols = slice(c * HALF, (c + 1) * HALF)
                at_edge = lane < 2 if c == 0 else lane >= 126
                more = jnp.where(at_edge, edge, 0.0)
                more = more + jnp.where(((row == 5) | (row == 6)) & on_top, turn(fold[c], 5 - 2 * l, 0), 0.0)
                ready.append((j, cols, pre_ref[j, :, cols] + jnp.where(depth[c] > j, more, 0.0)))
        return ready

    def several(step, carry):
        ready = []
        for part in range(TOGETHER):
            ready += quad_values(step * TOGETHER + part, 4)
        for j, cols, value in ready:
            put(j, cols, value)
        if after is not None:
            after(step * TOGETHER + TOGETHER - 1)
        return carry

    lax.fori_loop(0, FULL_QUADS // TOGETHER, several, 0)
    for j, cols, value in quad_values(FULL_QUADS, TAIL):
        put(j, cols, value)
    if after is not None:
        after(FULL_QUADS)


def start_ahead(quad, levels_copy):
    @pl.when(quad + AHEAD < FULL_QUADS)
    def _():
        levels_copy(quad + AHEAD, 4).start()

    @pl.when(quad + AHEAD == FULL_QUADS)
    def _():
        levels_copy(FULL_QUADS, TAIL).start()


def first_kernel(lam_hbm, inv_hbm, se_hbm, me_hbm, sn_hbm, mn_hbm, depth_hbm,
                 g_ref, slots_hbm, north_ref, south_ref,
                 lam, inverse, se, me, sn, mn, depth_ref, fold_scr, lon_scr, lonc_scr,
                 flipped_scr, rim_scr, small_sem, sem, slot_sem, rim_sem):
    small = [pltpu.make_async_copy(src, dst, small_sem.at[i])
             for i, (src, dst) in enumerate([(depth_hbm, depth_ref), (lam_hbm, lam), (sn_hbm, sn),
                                             (mn_hbm, mn), (se_hbm, se), (me_hbm, me)])]

    def levels_copy(quad, count):
        part = pl.ds(quad * 4, count)
        return pltpu.make_async_copy(inv_hbm.at[:, part], inverse.at[:, part], sem.at[quad])

    small[0].start()
    small[1].start()
    levels_copy(0, 4).start()
    levels_copy(1, 4).start()
    for copy in small[2:]:
        copy.start()
    for quad in range(2, AHEAD):
        levels_copy(quad, 4).start()
    small[0].wait()
    small[1].wait()
    depth = depth_ref[...]

    def mask(k, carry):
        lam[k] = jnp.where(depth > k, lam[k], 0.0)
        return carry

    lax.fori_loop(0, LEV, mask, 0, unroll=5)
    for copy in small[2:]:
        copy.wait()

    def pack(quad, count, beside):
        pack_quad(quad, count, g_ref, sn, mn, se, me, north_ref, south_ref, fold_scr, lon_scr, lonc_scr, True, beside)

    sum_quads(inverse, lam, depth, g_ref, levels_copy, pack)
    for part, (ref, side) in enumerate(((lon_scr, 1), (lonc_scr, 0), (lonc_scr, 2))):
        g_ref[LEV + part] = jnp.concatenate([ref[side, 0], ref[side, 1]], axis=1)
    fill_sends(slots_hbm, fold_scr, lon_scr, lonc_scr, flipped_scr, rim_scr, slot_sem, rim_sem)


def second_kernel(pre_ref, fold_ref, near_ref, far1_ref, far2_ref, far3_ref,
                  inv_hbm, sn_ref, mn_ref, depth_ref,
                  g_ref, slots_hbm, north_ref, south_ref,
                  lam, inverse, fold_scr, lon_scr, flipped_scr, rim_scr, sem, slot_sem, rim_sem):
    def levels_copy(quad, count):
        part = pl.ds(quad * 4, count)
        return pltpu.make_async_copy(inv_hbm.at[:, part], inverse.at[:, part], sem.at[quad])

    for quad in range(AHEAD):
        levels_copy(quad, 4).start()

    def put(j, cols, value):
        lam[j, :, cols] = value

    west_s, east_s = lon_rims(near_ref, far1_ref, far3_ref, 1)
    west_m, _ = lon_rims(near_ref, far1_ref, far3_ref, 2)
    for part, tile in enumerate((west_s, west_m, east_s)):
        g_ref[OWN + part] = tile
    add_fold(pre_ref, fold_ref, near_ref, (far1_ref, far2_ref, far3_ref), (west_s, west_m, east_s), depth_ref, put)
    depth = depth_ref[...]

    def pack(quad, count, beside):
        pack_quad(quad, count, g_ref, sn_ref, mn_ref, None, None, north_ref, south_ref, fold_scr, lon_scr, None, False,
                  beside)

    sum_quads(inverse, lam, depth, g_ref, levels_copy, pack)
    g_ref[LEV] = jnp.concatenate([lon_scr[1, 0], lon_scr[1, 1]], axis=1)
    for part in range(LEV + 1, OWN):
        g_ref[part] = pre_ref[part]
    fill_sends(slots_hbm, fold_scr, lon_scr, None, flipped_scr, rim_scr, slot_sem, rim_sem)


def last_kernel(pre_ref, fold_ref, near_ref, far1_ref, far2_ref, far3_ref,
                depth_ref, out_hbm, total, sem):
    copies = [pltpu.make_async_copy(total.at[pl.ds(start, size)], out_hbm.at[pl.ds(start, size)], sem.at[i])
              for i, (start, size) in enumerate(((0, 24), (24, 24), (48, 27)))]

    def put(j, cols, value):
        total[j, :, cols] = value

    def after(quad):
        for i, last in enumerate((5, 11, FULL_QUADS)):
            @pl.when(quad == last)
            def _(copy=copies[i]):
                copy.start()

    add_fold(pre_ref, fold_ref, near_ref, (far1_ref, far2_ref, far3_ref),
             [pre_ref[part] for part in range(OWN, EXT)], depth_ref, put, after)
    for copy in copies:
        copy.wait()


def relay_kernel(fold_ref, near_ref, *refs):
    fars = lax.axis_size("far")
    my_far = lax.axis_index("far")
    my_near = lax.axis_index("near")
    far1_ref, _, far3_ref = refs[-3:]
    for ref, slot in ((far1_ref, lax.rem(my_near + NEAR - 1, NEAR)), (far3_ref, lax.rem(my_near + 1, NEAR))):
        for part in range(QUADS, ref.shape[0]):
            ref[part] = near_ref[slot, part]

    @pl.when(lax.axis_index("lat") == lax.axis_size("lat") - 1)
    def _():
        for step, out_ref in enumerate(refs[-3:]):
            target = lax.rem(my_far + step + 1, fars)
            _, near = place_of(fold_ref[target * NEAR + my_near])
            for quad in range(QUADS):
                out_ref[quad] = near_ref[near, quad]


def shaped(shape, dtype):
    return jax.ShapeDtypeStruct(shape, dtype)


def per_device(lam, inverse, se, me, sn, mn, depth, fold_block):
    field = (LEV, ROWS, COLS)
    extended = (EXT, ROWS, COLS)
    lats = lax.axis_size("lat")
    count = lax.axis_size("far") * NEAR
    lon = ("far", "near")
    vmem = pl.BlockSpec(memory_space=pltpu.VMEM)
    hbm = pl.BlockSpec(memory_space=pltpu.HBM)
    smem = pl.BlockSpec(memory_space=pltpu.SMEM)
    coefs = [se, me, sn, mn]
    lon_scr = pltpu.VMEM((2, 2, ROWS, HALF), F32)
    fold_scr = pltpu.VMEM((20, ROWS, COLS), F32)
    inverse_scr = pltpu.VMEM((LEV,) + field, BF16)
    quad_sems = pltpu.SemaphoreType.DMA((QUADS,))
    slot_sems = [pltpu.SemaphoreType.DMA((NEAR,)), pltpu.SemaphoreType.DMA((2,))]
    work = 2 * LEV * LEV * ROWS * COLS
    mib = 1024 * 1024
    block = (QUADS, ROWS, COLS)

    def cost(bytes_accessed):
        return pl.CostEstimate(flops=work, bytes_accessed=bytes_accessed, transcendentals=0)

    def limit(size):
        return pltpu.CompilerParams(vmem_limit_bytes=size * mib)

    def sends(north, south, parts):
        return [shaped((NEAR, QUADS + parts, ROWS, COLS), BF16), shaped((north,) + block, BF16),
                shaped((south,) + block, BF16)]

    def staging(parts):
        return [pltpu.VMEM(block, BF16), pltpu.VMEM((2, parts, ROWS, COLS), BF16)]

    g1, *sent1 = pl.pallas_call(
        first_kernel,
        in_specs=[hbm] * 7,
        out_specs=[vmem, hbm, vmem, vmem],
        out_shape=[shaped(extended, F32)] + sends(2, 1, 3),
        scratch_shapes=[pltpu.VMEM(field, F32), inverse_scr] + [pltpu.VMEM(field, BF16)] * 4
        + [pltpu.VMEM((ROWS, COLS), jnp.int32), fold_scr, lon_scr, pltpu.VMEM((3, 2, ROWS, HALF), F32)]
        + staging(3) + [pltpu.SemaphoreType.DMA((6,)), quad_sems] + slot_sems,
        compiler_params=limit(62),
        cost_estimate=cost(work),
        name="vertical_first",
    )(lam, inverse, *coefs, depth)

    def ring(size, shift):
        return [(i, (i + shift) % size) for i in range(size)]

    def exchange(g, slots, north, south, *carried):
        near = lax.all_to_all(slots, "near", 0, 0, tiled=True)
        rims = [lax.ppermute(north, "lat", ring(lats, 1)), lax.ppermute(south, "lat", ring(lats, -1))]
        parts = slots.shape[1]
        held = len(carried)
        g, north, south, *rest = pl.pallas_call(
            relay_kernel,
            in_specs=[smem] + [vmem] * (4 + held),
            out_specs=[vmem] * (6 + held),
            out_shape=[shaped(extended, F32)] + [shaped(part.shape, BF16) for part in (*rims, *carried)]
            + [shaped((size, ROWS, COLS), BF16) for size in (parts, QUADS, parts)],
            input_output_aliases={2 + i: i for i in range(3 + held)},
            compiler_params=limit(4),
            cost_estimate=cost(work),
            name="relay",
        )(fold_block, near, g, *rims, *carried)
        carried, fars = rest[:held], rest[held:]
        far = [lax.ppermute(part, lon, ring(count, NEAR * (step + 1))) for step, part in enumerate(fars)]
        return g, (north, south), (near, *far), carried

    def stencil(g, rims, north_c):
        return pl.pallas_call(
            transposed_h,
            in_specs=[vmem] * 9,
            out_specs=vmem,
            out_shape=shaped(extended, F32),
            compiler_params=limit(4),
            cost_estimate=cost(work),
            name="horizontal",
        )(g, *coefs, depth, *rims, north_c)

    g1, rims1, folds1, _ = exchange(g1, *sent1)
    pre1 = stencil(g1, rims1, rims1[0])

    g2, *sent2 = pl.pallas_call(
        second_kernel,
        in_specs=[vmem, smem] + [vmem] * 4 + [hbm] + [vmem] * 3,
        out_specs=[vmem, hbm, vmem, vmem],
        out_shape=[shaped(extended, F32)] + sends(1, 1, 1),
        scratch_shapes=[pltpu.VMEM(field, F32), inverse_scr, fold_scr, lon_scr] + staging(1) + [quad_sems] + slot_sems,
        compiler_params=limit(36),
        cost_estimate=cost(work),
        name="vertical_second",
    )(pre1, fold_block, *folds1, inverse, sn, mn, depth)

    g2, rims2, folds2, (north_c,) = exchange(g2, *sent2, rims1[0])
    pre2 = stencil(g2, rims2, north_c)

    return pl.pallas_call(
        last_kernel,
        in_specs=[vmem, smem] + [vmem] * 5,
        out_specs=hbm,
        out_shape=shaped(field, F32),
        scratch_shapes=[pltpu.VMEM(field, F32), pltpu.SemaphoreType.DMA((3,))],
        compiler_params=limit(4),
        name="add_fold",
    )(pre2, fold_block, *folds2, depth)


def solution(mesh):
    lons, lats = mesh.devices.shape
    split = jax.sharding.Mesh(mesh.devices.reshape(lons // NEAR, NEAR, lats), ("far", "near", "lat"))
    lon = ("far", "near")
    field = P(None, "lat", lon)
    return jax.shard_map(
        per_device,
        mesh=split,
        in_specs=(field, P(None, None, "lat", lon), field, field, field, field, P("lat", lon), P()),
        out_specs=field,
        check_vma=False,
    )
```
